256 devices in a mesh: bin: 16 (over y_lo, z), sky: 16 (over x, y_hi, core).
Axes of the slice: x: 4, y: 4 (y_hi: 2, y_lo: 2; y = y_hi * 2 + y_lo), z: 8, core: 2. Of those that a mesh axis runs over, the one named last changes fastest.
Arguments:
- lensing_maps: bfloat16 [16, 128, 8192], P('bin', 'sky')
- filter_taps: float32 [5, 17], replicated, may hold values from -1.5 to 1.5
- survey_mask: int32 [16, 64], P('sky'), may hold values 0 or 1
- bin_pairs: int32 [136, 2], replicated, may hold values from 0 to 15, as said below
- target_corr: float32 [136, 5, 4], replicated, may hold values from -3 to 3
- pair_weight: float32 [136, 5, 4], replicated, may hold values from 0.3 to 3
Outputs:
- corr_table: float32 [136, 5, 4], replicated
- map_gradient: float32 [16, 128, 8192], P('bin', 'sky')
The draws below stay inside these ranges and needn't reach their ends.
Inputs may be any that keep to these rules, and one draw needn't show every extreme that they name: `bin_pairs`: every unordered pair of the 16 bins, a bin with itself included, is listed exactly once; the order of the list and of the two bins in a row vary.
All inputs are finite; a program needn't handle non-finite values. No bound on the sum of `survey_mask` on one device may be relied on, other than what follows from the above.
Results may differ from the reference program's by a relative error of at most 0.0015.
Values may be sent and summed in bfloat16 or wider, within the bound.
No kernel may reach another device: no remote copies, remote signals or barrier semaphores. Data moves between devices by JAX's collectives and lax.ppermute only.
A program may use at most 64 MiB of HBM per device.

```python
import math
import jax
import jax.numpy as jnp
import numpy as np
from jax import lax

BINS = 16
PAIRS = 136
SCALES = 5
HALF = 8
LAGS = 4
NY = 8192
NX = 128


def draw_lensing_maps(key, part):
    amplitude = jax.random.uniform(jax.random.fold_in(key, 3), (BINS, 1, 1), jnp.float32, 0.5, 0.95)
    shared = jax.random.normal(jax.random.fold_in(key, 1), (NX, NY), jnp.float32)
    single = jax.random.normal(jax.random.fold_in(key, 2), (BINS, NX, NY), jnp.float32)
    mixed = amplitude * shared[None] + jnp.sqrt(1.0 - amplitude * amplitude) * single
    return mixed.astype(jnp.bfloat16)


def draw_bin_pairs(key, part):
    upper_row, upper_col = np.triu_indices(BINS)
    ordering = jax.random.permutation(jax.random.fold_in(key, 11), PAIRS)
    flipped = jax.random.randint(jax.random.fold_in(key, 12), (PAIRS,), 0, 2)
    left_bin = jnp.asarray(upper_row, jnp.int32)[ordering]
    right_bin = jnp.asarray(upper_col, jnp.int32)[ordering]
    first_bin = jnp.where(flipped == 1, right_bin, left_bin)
    second_bin = jnp.where(flipped == 1, left_bin, right_bin)
    return jnp.stack([first_bin, second_bin], axis=1).astype(jnp.int32)


def with_ends(entries, own_key, least, largest):
    longest = entries.shape.index(max(entries.shape))
    spots = []
    for shift in (0, 1):
        where = [jax.random.randint(jax.random.fold_in(own_key, axis), (), 0, length) for axis, length in enumerate(entries.shape)]
        where[longest] = (where[longest] + shift) % entries.shape[longest]
        spots.append(tuple(where))
    return entries.at[spots[0]].set(least).at[spots[1]].set(largest)


def gaussian(own_key, extent, deviation, limit, held_as=jnp.bfloat16):
    entries = deviation * jax.random.normal(own_key, extent, jnp.float32)
    return jnp.clip(entries, min=-limit, max=limit).astype(held_as)


def setup_inputs(seed: int = 0) -> dict:
    arg_keys = jax.random.split(jax.random.key(seed), 7)
    return {
        "lensing_maps": draw_lensing_maps(jax.random.fold_in(arg_keys[6], 71), 0),
        "filter_taps": gaussian(arg_keys[1], (SCALES, 2 * HALF + 1), (2 * HALF + 1) ** -0.5, 1.5, jnp.float32),
        "survey_mask": with_ends((jax.random.randint(arg_keys[2], (NX // 8, NY // 128), 0, 4) < 3).astype(jnp.int32), jax.random.fold_in(arg_keys[2], 1), 0, 1),
        "bin_pairs": draw_bin_pairs(jax.random.fold_in(arg_keys[6], 71), 0),
        "target_corr": gaussian(arg_keys[4], (PAIRS, SCALES, LAGS), 0.5, 3.0, jnp.float32),
        "pair_weight": jnp.clip(jnp.exp(jax.random.uniform(arg_keys[5], (PAIRS, SCALES, LAGS), jnp.float32, math.log(0.3), math.log(3.0))), 0.3, 3.0),
    }


HIGH = lax.Precision.HIGHEST


def expand_mask(survey_mask):
    values = survey_mask.astype(jnp.float32)
    tiles_x, tiles_y = values.shape
    return jnp.broadcast_to(values[:, None, :, None], (tiles_x, 8, tiles_y, 128)).reshape(tiles_x * 8, tiles_y * 128)


def smooth(haloed, filter_taps, row_count):
    tap_count = filter_taps.shape[1]
    half_width = (tap_count - 1) // 2
    widened = haloed.astype(jnp.float32)
    across = filter_taps[:, 0, None, None] * widened[None, 0:row_count]
    for a in range(1, tap_count):
        across = across + filter_taps[:, a, None, None] * widened[None, a:a + row_count]
    padded = jnp.pad(across, ((0, 0), (0, 0), (half_width, half_width)))
    col_count = widened.shape[1]
    result = filter_taps[:, 0, None, None] * padded[:, :, 0:col_count]
    for c in range(1, tap_count):
        result = result + filter_taps[:, c, None, None] * padded[:, :, c:c + col_count]
    return result.astype(jnp.bfloat16)


def lagged(left_maps, right_maps, pixmask, lag_count):
    col_count = left_maps.shape[2]
    columns = []
    for offset in range(lag_count):
        joint_mask = pixmask[:, :col_count - offset] * pixmask[:, offset:]
        product = left_maps[:, :, :col_count - offset].astype(jnp.float32) * right_maps[:, :, offset:].astype(jnp.float32) * joint_mask[None]
        columns.append(jnp.sum(product, axis=(1, 2)))
    return jnp.stack(columns, axis=1)


def adjoint_lags(partner, ahead_w, behind_w, pixmask):
    col_count = partner.shape[2]
    widened = partner.astype(jnp.float32)
    totals = jnp.zeros(partner.shape, jnp.float32)
    for offset in range(ahead_w.shape[1]):
        joint_mask = pixmask[:, :col_count - offset] * pixmask[:, offset:]
        front = jnp.pad(joint_mask[None] * widened[:, :, offset:], ((0, 0), (0, 0), (0, offset)))
        back = jnp.pad(joint_mask[None] * widened[:, :, :col_count - offset], ((0, 0), (0, 0), (offset, 0)))
        totals = totals + ahead_w[:, offset, None, None] * front + behind_w[:, offset, None, None] * back
    return totals


def adjoint_cols(grads, filter_taps):
    tap_count = filter_taps.shape[1]
    half_width = (tap_count - 1) // 2
    col_count = grads.shape[2]
    padded = jnp.pad(grads, ((0, 0), (0, 0), (half_width, half_width)))
    result = filter_taps[:, tap_count - 1, None, None] * padded[:, :, 0:col_count]
    for c in range(1, tap_count):
        result = result + filter_taps[:, tap_count - 1 - c, None, None] * padded[:, :, c:c + col_count]
    return result


def adjoint_rows(widened, filter_taps, row_count):
    tap_count = filter_taps.shape[1]
    result = filter_taps[:, tap_count - 1, None, None] * widened[:, 0:row_count]
    for a in range(1, tap_count):
        result = result + filter_taps[:, tap_count - 1 - a, None, None] * widened[:, a:a + row_count]
    return jnp.sum(result, axis=0)


def reference(lensing_maps, filter_taps, survey_mask, bin_pairs, target_corr, pair_weight):
    half_width = (filter_taps.shape[1] - 1) // 2
    pixmask = expand_mask(survey_mask)
    lag_count = pair_weight.shape[2]
    inverse_area = 1.0 / (NX * NY)

    def filter_one(one_map):
        return smooth(jnp.pad(one_map, ((half_width, half_width), (0, 0))), filter_taps, NX)

    filtered = lax.map(filter_one, lensing_maps)

    def row_of(left_maps):
        def with_partner(partner):
            return lagged(left_maps, partner, pixmask, lag_count) * inverse_area
        return lax.map(with_partner, filtered)

    pair_table = lax.map(row_of, filtered)
    indices = jnp.arange(BINS, dtype=jnp.int32)
    left_hot = (bin_pairs[:, 0:1] == indices[None, :]).astype(jnp.float32)
    right_hot = (bin_pairs[:, 1:2] == indices[None, :]).astype(jnp.float32)
    corr_table = jnp.einsum('pi,pj,ijsl->psl', left_hot, right_hot, pair_table, precision=HIGH)
    pair_grad = pair_weight * (corr_table - target_corr)
    table_grad = jnp.einsum('pi,pj,psl->ijsl', left_hot, right_hot, pair_grad, precision=HIGH)

    def grad_one(inputs):
        row_grad, col_grad = inputs

        def gather_term(totals, terms):
            partner, ahead_w, behind_w = terms
            return totals + adjoint_lags(partner, ahead_w, behind_w, pixmask), None

        totals, _ = lax.scan(gather_term, jnp.zeros((SCALES, NX, NY), jnp.float32), (filtered, row_grad, col_grad))
        col_pass = adjoint_cols(totals, filter_taps)
        widened = jnp.pad(col_pass, ((0, 0), (half_width, half_width), (0, 0)))
        return adjoint_rows(widened, filter_taps, NX)

    map_gradient = lax.map(grad_one, (table_grad, jnp.transpose(table_grad, (1, 0, 2, 3))))
    return (corr_table, map_gradient)
```

```python
import jax
import jax.numpy as jnp
from jax import lax
from jax.experimental import pallas as pl
from jax.experimental.pallas import tpu as pltpu
from jax.sharding import PartitionSpec as P

F32 = jnp.float32
BF16 = jnp.bfloat16
HIGH = lax.Precision.HIGHEST

BINS = 16
SCALES = 5
TAPS = 17
LAGS = 4
ROWS = 8
OWN = 512
LANE = 128
EDGE = 64
WIN = OWN + 2 * EDGE
RAW = OWN + 4 * EDGE
XB = ROWS * BINS


def full(shape):
    return pl.BlockSpec(shape, lambda *_: (0,) * len(shape))


def per_scale(shape):
    return pl.BlockSpec((1,) + shape, lambda s: (s,) + (0,) * len(shape))


SMEM = pl.BlockSpec(memory_space=pltpu.SMEM)


def split2(v):
    hi = v.astype(BF16)
    return hi, (v - hi.astype(F32)).astype(BF16)


def iota(shape, dim):
    return lax.broadcasted_iota(jnp.int32, shape, dim)


def windows_kernel(x_ref, out_ref):
    x = x_ref[...].astype(F32)
    count = x.shape[1] // OWN
    blank = jnp.zeros((ROWS, LANE), F32)

    def window(b):
        parts = []
        if b == 0:
            parts.append(blank)
        low = max(b * OWN - LANE, 0)
        high = min((b + 1) * OWN + LANE, x.shape[1])
        parts.append(x[:, low:high])
        if b == count - 1:
            parts.append(blank)
        return jnp.concatenate(parts, axis=1) if len(parts) > 1 else parts[0]

    for p in range(count // 2):
        pair = jnp.concatenate([window(2 * p), window(2 * p + 1)], axis=0)
        out_ref[2 * ROWS * p : 2 * ROWS * (p + 1), :] = pair.astype(BF16)


def matrices_kernel(taps_ref, r_ref, w_ref, wa_ref, ra_ref):
    q = iota((XB, 3 * XB), 0)
    n = iota((XB, 3 * XB), 1)
    row_tap = jnp.where(q % BINS == (n % XB) // ROWS, n % ROWS - q // BINS + ROWS * (n // XB), -1)
    n = iota((2 * LANE, LANE), 0)
    o = iota((2 * LANE, LANE), 1)
    col_tap = n - o - 56
    col_adj_tap = o + 72 - n
    q = iota((3 * XB, XB), 0)
    n = iota((3 * XB, XB), 1)
    row_adj_tap = jnp.where(
        (q % XB) // ROWS == n % BINS, q % ROWS - n // BINS + ROWS * (q // XB), -1
    )

    def spread(index, s):
        value = jnp.zeros(index.shape, F32)
        for a in range(TAPS):
            value = jnp.where(index == a, taps_ref[s, a], value)
        return split2(value)

    def one(s, carry):
        hi, lo = spread(row_tap, s)
        r_ref[s, 0:XB, :] = hi
        r_ref[s, XB : 2 * XB, :] = lo
        hi, lo = spread(col_tap, s)
        w_ref[s, :, 0:LANE] = hi
        w_ref[s, :, LANE : 2 * LANE] = lo
        hi, lo = spread(col_adj_tap, s)
        wa_ref[s, :, 0:LANE] = hi
        wa_ref[s, :, LANE : 2 * LANE] = lo
        hi, lo = spread(row_adj_tap, s)
        at = pl.ds(pl.multiple_of(s * XB, XB), XB)
        ra_ref[0, :, at] = hi
        ra_ref[1, :, at] = lo
        return carry

    lax.fori_loop(0, SCALES, one, 0)


def window_mask(mask_ref):
    b = lax.axis_index("bin")
    tiles = mask_ref.shape[1]
    lane = iota((1, LANE), 1)

    def tile(t):
        value = mask_ref[0, jnp.clip(t, 0, tiles - 1)]
        return jnp.where((t >= 0) & (t < tiles), value, 0)

    first = b * (OWN // LANE)
    parts = [
        jnp.where(lane < EDGE, tile(first + f - 1), tile(first + f)) for f in range(WIN // LANE)
    ]
    return jnp.concatenate(parts, axis=1)


def banded(v, w, tiles):
    parts = split2(v)
    stacked = jnp.concatenate(
        [p[:, LANE * f : LANE * (f + 2)] for p in parts for f in range(tiles)], axis=0
    )
    d = jnp.dot(stacked, w, preferred_element_type=F32)
    d = d[:, :LANE] + d[:, LANE:]
    return [d[XB * f : XB * (f + 1)] + d[XB * (tiles + f) : XB * (tiles + f + 1)] for f in range(tiles)]


def forward_kernel(mask_ref, up_ref, own_ref, down_ref, r_ref, w_ref, g_ref, table_ref, raw_ref):
    s = pl.program_id(0)

    @pl.when(s == 0)
    def _():
        raw_ref[0:XB, :] = up_ref[...]
        raw_ref[XB : 2 * XB, :] = own_ref[...]
        raw_ref[2 * XB : 3 * XB, :] = down_ref[...]

    d = jnp.dot(r_ref[0], raw_ref[...], preferred_element_type=F32)
    row_pass = d[:XB] + d[XB:]
    tiles = banded(row_pass, w_ref[0], WIN // LANE)
    mask = window_mask(mask_ref)
    filtered = jnp.concatenate(tiles, axis=1).astype(BF16).astype(F32)
    g = jnp.where(mask != 0, filtered, 0.0)
    for l in range(LAGS):
        for side in range(2):
            steps = (WIN - l) % WIN if side == 0 else l
            moved = pltpu.roll(g, steps, 1) if steps else g
            at = (side * LAGS + l) * BINS
            g_ref[0, :, at : at + BINS, :] = moved.astype(BF16).reshape(ROWS, BINS, WIN)
    lane = iota((XB, WIN), 1)
    left = jnp.where((lane >= EDGE) & (lane < EDGE + OWN), g, 0.0).astype(BF16)
    right = g_ref[0, :, 0 : LAGS * BINS, :].reshape(ROWS * LAGS * BINS, WIN)
    cross = lax.dot_general(left, right, (((1,), (1,)), ((), ())), preferred_element_type=F32)
    width = LAGS * BINS
    lane = iota((BINS, ROWS * width), 1)
    total = jnp.zeros((BINS, ROWS * width), F32)
    for x in range(ROWS):
        total = total + jnp.where(lane // width == x, cross[BINS * x : BINS * (x + 1)], 0.0)
    total = sum(total[:, LANE * i : LANE * (i + 1)] for i in range(ROWS * width // LANE))
    total = total[:, :width] + total[:, width:]
    for i in range(SCALES):

        @pl.when(s == i)
        def _():
            table_ref[:, width * i : width * (i + 1)] = total


def backward_kernel(
    inverse_area,
    mask_ref, table_ref, pairs_ref, target_ref, weight_ref, g_ref, wa_ref, ra_ref,
    corr_ref, up_ref, own_ref, down_ref, a_ref, hi_ref, lo_ref,
):
    s = pl.program_id(0)
    width = LAGS * BINS
    total = SCALES * width

    @pl.when(s == 0)
    def _():
        count = pairs_ref.shape[0]
        first = pairs_ref[:, 0:1]
        second = pairs_ref[:, 1:2]
        bins = iota((count, BINS), 1)
        left = (first == bins).astype(F32)
        right = (second == bins).astype(F32)
        bins = iota((count, total), 1) % BINS
        left_wide = (first == bins).astype(F32)
        right_wide = (second == bins).astype(F32)
        entries = SCALES * LAGS
        expand = (iota((entries, total), 1) // BINS == iota((entries, total), 0)).astype(F32)

        def dot(a, b, dims):
            return lax.dot_general(a, b, (dims, ((), ())), precision=HIGH, preferred_element_type=F32)

        table = table_ref[...] * inverse_area
        chosen = dot(left, table, ((1,), (0,))) * right_wide
        corr = dot(chosen, expand, ((1,), (1,)))
        corr_ref[...] = corr
        grad = weight_ref[...] * (corr - target_ref[...])
        grad_wide = dot(grad, expand, ((1,), (0,)))
        ahead = dot(left, grad_wide * right_wide, ((0,), (0,)))
        behind = dot(right, grad_wide * left_wide, ((0,), (0,)))
        for i in range(SCALES):
            at = slice(width * i, width * (i + 1))
            both = jnp.concatenate([ahead[:, at], behind[:, at]], axis=1)
            hi, lo = split2(both)
            a_ref[i, 0:BINS, :] = hi
            a_ref[i, BINS : 2 * BINS, :] = lo

    mix = a_ref[s]
    mask = window_mask(mask_ref)
    rows = []
    for x in range(ROWS):
        d = jnp.dot(mix, g_ref[0, x], preferred_element_type=F32)
        rows.append(jnp.where(mask != 0, d[:BINS] + d[BINS:], 0.0))
    tiles = banded(jnp.concatenate(rows, axis=0), wa_ref[0], OWN // LANE)
    at = pl.ds(pl.multiple_of(s * XB, XB), XB)
    for c, tile in enumerate(tiles):
        hi, lo = split2(tile)
        hi_ref[at, LANE * c : LANE * (c + 1)] = hi
        lo_ref[at, LANE * c : LANE * (c + 1)] = lo

    @pl.when(s == SCALES - 1)
    def _():
        out = (
            jnp.dot(ra_ref[0], hi_ref[...], preferred_element_type=F32)
            + jnp.dot(ra_ref[0], lo_ref[...], preferred_element_type=F32)
            + jnp.dot(ra_ref[1], hi_ref[...], preferred_element_type=F32)
        )
        up_ref[...] = out[0:XB]
        own_ref[...] = out[XB : 2 * XB]
        down_ref[...] = out[2 * XB : 3 * XB]


def struct(shape, dtype):
    return jax.ShapeDtypeStruct(shape, dtype)


LIMIT = pltpu.CompilerParams(vmem_limit_bytes=48 * 1024 * 1024)


def total_over(value, axis):
    count = lax.axis_size(axis)
    copies = jnp.broadcast_to(value[None], (count,) + value.shape)
    return jnp.sum(lax.all_to_all(copies, axis, 0, 0, tiled=True), axis=0)


def per_device(lensing_maps, filter_taps, survey_mask, bin_pairs, target_corr, pair_weight):
    strip = lensing_maps[0]
    rows, cols = strip.shape
    sky = lax.axis_size("sky")
    pairs = bin_pairs.shape[0]
    inverse_area = 1.0 / (rows * sky * cols)
    down_perm = [(i, i + 1) for i in range(sky - 1)]
    up_perm = [(i + 1, i) for i in range(sky - 1)]

    windows = pl.pallas_call(
        windows_kernel,
        out_shape=struct((XB, RAW), BF16),
        name="windows",
    )(strip)
    own = lax.all_to_all(windows, "bin", 0, 0, tiled=True)
    r, w, wa, ra = pl.pallas_call(
        matrices_kernel,
        in_specs=[SMEM],
        out_shape=(
            struct((SCALES, 2 * XB, 3 * XB), BF16),
            struct((SCALES, 2 * LANE, 2 * LANE), BF16),
            struct((SCALES, 2 * LANE, 2 * LANE), BF16),
            struct((2, 3 * XB, SCALES * XB), BF16),
        ),
        compiler_params=LIMIT,
        cost_estimate=pl.CostEstimate(flops=20_000_000, bytes_accessed=4_000_000, transcendentals=0),
        name="matrices",
    )(filter_taps)
    above = lax.ppermute(own, "sky", down_perm)
    below = lax.ppermute(own, "sky", up_perm)
    width = LAGS * BINS
    g, partial = pl.pallas_call(
        forward_kernel,
        grid=(SCALES,),
        in_specs=[
            SMEM,
            full((XB, RAW)),
            full((XB, RAW)),
            full((XB, RAW)),
            per_scale((2 * XB, 3 * XB)),
            per_scale((2 * LANE, 2 * LANE)),
        ],
        out_specs=[per_scale((ROWS, 2 * width, WIN)), full((BINS, SCALES * width))],
        out_shape=(
            struct((SCALES, ROWS, 2 * width, WIN), BF16),
            struct((BINS, SCALES * width), F32),
        ),
        scratch_shapes=[pltpu.VMEM((3 * XB, RAW), BF16)],
        compiler_params=LIMIT,
        name="forward",
    )(survey_mask, above, own, below, r, w)
    table = total_over(total_over(partial, "sky"), "bin")
    corr, up, mid, down = pl.pallas_call(
        lambda *refs: backward_kernel(inverse_area, *refs),
        grid=(SCALES,),
        in_specs=[
            SMEM,
            full((BINS, SCALES * width)),
            full((pairs, 2)),
            full((pairs, SCALES * LAGS)),
            full((pairs, SCALES * LAGS)),
            per_scale((ROWS, 2 * width, WIN)),
            per_scale((2 * LANE, 2 * LANE)),
            full((2, 3 * XB, SCALES * XB)),
        ],
        out_specs=[full((pairs, SCALES * LAGS))] + [full((XB, OWN))] * 3,
        out_shape=(struct((pairs, SCALES * LAGS), F32),) + (struct((XB, OWN), F32),) * 3,
        scratch_shapes=[
            pltpu.VMEM((SCALES, 2 * BINS, 2 * width), BF16),
            pltpu.VMEM((SCALES * XB, OWN), BF16),
            pltpu.VMEM((SCALES * XB, OWN), BF16),
        ],
        compiler_params=LIMIT,
        name="backward",
    )(
        survey_mask,
        table,
        bin_pairs,
        target_corr.reshape(pairs, SCALES * LAGS),
        pair_weight.reshape(pairs, SCALES * LAGS),
        g,
        wa,
        ra,
    )
    from_below = lax.ppermute(up, "sky", up_perm)
    from_above = lax.ppermute(down, "sky", down_perm)
    tile_grad = mid + from_below + from_above
    back = lax.all_to_all(tile_grad, "bin", 0, 0, tiled=True)
    map_grad = jnp.transpose(back.reshape(BINS, rows, OWN), (1, 0, 2)).reshape(1, rows, cols)
    return (corr.reshape(target_corr.shape), map_grad)


def solution(mesh):
    placed = (P("bin", "sky", None), P(), P("sky", None), P(), P(), P())
    return jax.shard_map(
        per_device,
        mesh=mesh,
        in_specs=placed,
        out_specs=(P(), P("bin", "sky", None)),
        check_vma=False,
    )
```

```python
import jax
import jax.numpy as jnp
from jax import lax
from jax.experimental import pallas as pl
from jax.experimental.pallas import tpu as pltpu
from jax.sharding import PartitionSpec as P

F32 = jnp.float32
BF16 = jnp.bfloat16
HIGH = lax.Precision.HIGHEST

BINS = 16
SCALES = 5
TAPS = 17
LAGS = 4
ROWS = 8
OWN = 512
LANE = 128
EDGE = 64
WIN = OWN + 2 * EDGE
RAW = OWN + 4 * EDGE
XB = ROWS * BINS
WIDE = LAGS * BINS
TABLE = SCALES * WIDE
ENTRIES = SCALES * LAGS
PAIRS = 144
GROUPS = PAIRS // 8
PACK = 384


def full(shape):
    return pl.BlockSpec(shape, lambda *_: (0,) * len(shape))


def per_scale(shape):
    return pl.BlockSpec((1,) + shape, lambda s: (s,) + (0,) * len(shape))


SMEM = pl.BlockSpec(memory_space=pltpu.SMEM)


def split2(v):
    hi = v.astype(BF16)
    return hi, (v - hi.astype(F32)).astype(BF16)


def iota(shape, dim):
    return lax.broadcasted_iota(jnp.int32, shape, dim)


def windows_kernel(x_ref, out_ref):
    x = x_ref[...].astype(F32)
    count = x.shape[1] // OWN
    blank = jnp.zeros((ROWS, LANE), F32)

    def window(b):
        parts = []
        if b == 0:
            parts.append(blank)
        low = max(b * OWN - LANE, 0)
        high = min((b + 1) * OWN + LANE, x.shape[1])
        parts.append(x[:, low:high])
        if b == count - 1:
            parts.append(blank)
        return jnp.concatenate(parts, axis=1) if len(parts) > 1 else parts[0]

    for p in range(count // 2):
        pair = jnp.concatenate([window(2 * p), window(2 * p + 1)], axis=0)
        out_ref[2 * ROWS * p : 2 * ROWS * (p + 1), :] = pair.astype(BF16)


def matrices_kernel(
    taps_ref, mask_ref, pairs_ref, r_ref, w_ref, wa_ref, ra_ref, window_ref, left_ref, right_ref
):
    window_ref[...] = jnp.broadcast_to(window_mask(mask_ref), window_ref.shape)
    for c, out_ref in enumerate((left_ref, right_ref)):
        bins = iota(out_ref.shape, 1) % BINS
        out_ref[...] = (pairs_ref[:, c : c + 1] == bins).astype(F32).astype(BF16)
    q = iota((XB, 3 * XB), 0)
    n = iota((XB, 3 * XB), 1)
    row_tap = jnp.where(q % BINS == (n % XB) // ROWS, n % ROWS - q // BINS + ROWS * (n // XB), -1)
    n = iota((2 * LANE, LANE), 0)
    o = iota((2 * LANE, LANE), 1)
    col_tap = n - o - 56
    col_adj_tap = o + 72 - n
    q = iota((3 * XB, XB), 0)
    n = iota((3 * XB, XB), 1)
    row_adj_tap = jnp.where(
        (q % XB) // ROWS == n % BINS, q % ROWS - n // BINS + ROWS * (q // XB), -1
    )

    def spread(index, s):
        value = jnp.zeros(index.shape, F32)
        for a in range(TAPS):
            value = jnp.where(index == a, taps_ref[s, a], value)
        return split2(value)

    def one(s, carry):
        hi, lo = spread(row_tap, s)
        at = pl.ds(pl.multiple_of(s * XB, XB), XB)
        r_ref[at, 0 : 3 * XB] = hi
        r_ref[at, 3 * XB : 6 * XB] = lo
        hi, lo = spread(col_tap, s)
        w_ref[s, :, 0:LANE] = hi
        w_ref[s, :, LANE : 2 * LANE] = lo
        hi, lo = spread(col_adj_tap, s)
        wa_ref[s, :, 0:LANE] = hi
        wa_ref[s, :, LANE : 2 * LANE] = lo
        hi, lo = spread(row_adj_tap, s)
        ra_ref[0, :, at] = hi
        ra_ref[1, :, at] = lo
        return carry

    lax.fori_loop(0, SCALES, one, 0)


def window_mask(mask_ref):
    b = lax.axis_index("bin")
    tiles = mask_ref.shape[1]
    lane = iota((1, LANE), 1)

    def tile(t):
        value = mask_ref[0, jnp.clip(t, 0, tiles - 1)]
        return jnp.where((t >= 0) & (t < tiles), value, 0)

    first = b * (OWN // LANE)
    parts = [
        jnp.where(lane < EDGE, tile(first + f - 1), tile(first + f)) for f in range(WIN // LANE)
    ]
    return jnp.concatenate(parts, axis=1)


def banded(v, w, tiles):
    parts = split2(v)
    stacked = jnp.concatenate(
        [p[:, LANE * f : LANE * (f + 2)] for p in parts for f in range(tiles)], axis=0
    )
    d = jnp.dot(stacked, w, preferred_element_type=F32)
    d = d[:, :LANE] + d[:, LANE:]
    return [d[XB * f : XB * (f + 1)] + d[XB * (tiles + f) : XB * (tiles + f + 1)] for f in range(tiles)]


def spread_matrix():
    return (iota((ENTRIES, TABLE), 1) // BINS == iota((ENTRIES, TABLE), 0)).astype(F32).astype(BF16)


def forward_kernel(
    window_ref, up_ref, own_ref, down_ref, r_ref, w_ref, left_ref, right_ref,
    g_ref, out_ref, raw_ref, pass_ref,
):
    for i, ref in enumerate((up_ref, own_ref, down_ref) * 2):
        raw_ref[XB * i : XB * (i + 1), :] = ref[...]
    pass_ref[...] = jnp.dot(r_ref[...], raw_ref[...], preferred_element_type=F32)
    mask = window_ref[0:1, :] != 0
    lane = iota((XB, WIN), 1)
    inner = (lane >= EDGE) & (lane < EDGE + OWN)
    slab = iota((BINS, ROWS * WIDE), 1) // WIDE
    parts = []
    for s in range(SCALES):
        tiles = banded(pass_ref[XB * s : XB * (s + 1), :], w_ref[s], WIN // LANE)
        filtered = jnp.concatenate(tiles, axis=1).astype(BF16).astype(F32)
        g = jnp.where(mask, filtered, 0.0)
        g_ref[s] = g.astype(BF16)
        left = jnp.where(inner, g, 0.0).astype(BF16)
        right = jnp.concatenate(
            [
                (pltpu.roll(g, WIN - l, 1) if l else g).astype(BF16).reshape(ROWS, BINS, WIN)
                for l in range(LAGS)
            ],
            axis=1,
        ).reshape(ROWS * WIDE, WIN)
        cross = lax.dot_general(left, right, (((1,), (1,)), ((), ())), preferred_element_type=F32)
        total = jnp.zeros((BINS, ROWS * WIDE), F32)
        for x in range(ROWS):
            total = jnp.where(slab == x, cross[BINS * x : BINS * (x + 1)], total)
        total = sum(total[:, LANE * i : LANE * (i + 1)] for i in range(ROWS * WIDE // LANE))
        parts.append(total[:, :WIDE] + total[:, WIDE:])
    table = jnp.concatenate(parts, axis=1)
    pieces = []
    for _ in range(3):
        piece = table.astype(BF16)
        table = table - piece.astype(F32)
        chosen = jnp.dot(left_ref[:, 0:BINS], piece, preferred_element_type=F32)
        pieces.append(chosen.astype(BF16) * right_ref[...])
    entries = lax.dot_general(
        jnp.concatenate(pieces, axis=0), spread_matrix(), (((1,), (1,)), ((), ())),
        preferred_element_type=F32,
    )
    entries = entries[0:PAIRS] + (entries[PAIRS : 2 * PAIRS] + entries[2 * PAIRS :])
    packed = jnp.concatenate(
        [entries[8 * a : 8 * (a + 1)] for a in range(GROUPS)]
        + [jnp.zeros((8, PACK - GROUPS * ENTRIES), F32)],
        axis=1,
    )
    out_ref[...] = jnp.broadcast_to(packed[None], out_ref.shape)


def shifts_kernel(g_ref, out_ref):
    g = g_ref[0].astype(F32)
    for l in range(LAGS):
        for side in range(2):
            steps = (WIN - l) % WIN if side == 0 else l
            moved = pltpu.roll(g, steps, 1) if steps else g
            at = (side * LAGS + l) * BINS
            out_ref[0, :, at : at + BINS, :] = moved.astype(BF16).reshape(ROWS, BINS, WIN)


def backward_kernel(
    inverse_area,
    window_ref, sums_ref, target_ref, weight_ref, left_ref, right_ref, g_ref, wa_ref, ra_ref,
    corr_ref, up_ref, own_ref, down_ref, hi_ref, lo_ref,
):
    packed = sums_ref[0]
    for i in range(1, sums_ref.shape[0]):
        packed = packed + sums_ref[i]
    corr = inverse_area * jnp.concatenate(
        [packed[:, ENTRIES * a : ENTRIES * (a + 1)] for a in range(GROUPS)], axis=0
    )
    corr_ref[...] = corr
    grad = weight_ref[...] * (corr - target_ref[...])
    spread = spread_matrix()
    halves = []
    for piece in split2(grad):
        wide = jnp.dot(piece, spread, preferred_element_type=F32).astype(BF16)
        both = []
        for one, other in ((left_ref, right_ref), (right_ref, left_ref)):
            both.append(
                lax.dot_general(
                    one[:, 0:BINS], wide * other[...], (((0,), (0,)), ((), ())),
                    preferred_element_type=F32,
                )
            )
        halves.append(both)

    mask = window_ref[0:1, :] != 0
    for s in range(SCALES):
        at = slice(WIDE * s, WIDE * (s + 1))
        mix = jnp.concatenate(
            [jnp.concatenate([ahead[:, at], behind[:, at]], axis=1) for ahead, behind in halves],
            axis=0,
        )
        zero = jnp.zeros_like(mix)
        mix = jnp.concatenate(
            [jnp.concatenate([mix, zero], axis=1), jnp.concatenate([zero, mix], axis=1)], axis=0
        ).astype(BF16)
        rows = []
        for x in range(0, ROWS, 2):
            maps = g_ref[s, x : x + 2].reshape(2 * 2 * WIDE, WIN)
            d = jnp.dot(mix, maps, preferred_element_type=F32)
            for i in (0, 2 * BINS):
                rows.append(jnp.where(mask, d[i : i + BINS] + d[i + BINS : i + 2 * BINS], 0.0))
        tiles = banded(jnp.concatenate(rows, axis=0), wa_ref[s], OWN // LANE)
        for c, tile in enumerate(tiles):
            hi, lo = split2(tile)
            hi_ref[XB * s : XB * (s + 1), LANE * c : LANE * (c + 1)] = hi
            lo_ref[XB * s : XB * (s + 1), LANE * c : LANE * (c + 1)] = lo
    for i, ref in enumerate((up_ref, own_ref, down_ref)):
        at = slice(XB * i, XB * (i + 1))
        ref[...] = (
            jnp.dot(ra_ref[0, at, :], hi_ref[...], preferred_element_type=F32)
            + jnp.dot(ra_ref[0, at, :], lo_ref[...], preferred_element_type=F32)
            + jnp.dot(ra_ref[1, at, :], hi_ref[...], preferred_element_type=F32)
        )


def struct(shape, dtype):
    return jax.ShapeDtypeStruct(shape, dtype)


LIMIT = pltpu.CompilerParams(vmem_limit_bytes=48 * 1024 * 1024)


def cost(flops, moved):
    return pl.CostEstimate(flops=flops, bytes_accessed=moved, transcendentals=0)


def matrices(filter_taps, survey_mask, bin_pairs):
    pairs = jnp.pad(bin_pairs, ((0, PAIRS - bin_pairs.shape[0]), (0, 0)), constant_values=-1)
    return pl.pallas_call(
        matrices_kernel,
        in_specs=[SMEM, SMEM, pl.BlockSpec(memory_space=pltpu.VMEM)],
        out_shape=(
            struct((SCALES * XB, 6 * XB), BF16),
            struct((SCALES, 2 * LANE, 2 * LANE), BF16),
            struct((SCALES, 2 * LANE, 2 * LANE), BF16),
            struct((2, 3 * XB, SCALES * XB), BF16),
            struct((8, WIN), jnp.int32),
            struct((PAIRS, TABLE), BF16),
            struct((PAIRS, TABLE), BF16),
        ),
        compiler_params=LIMIT,
        cost_estimate=cost(20_000_000, 4_000_000),
        name="matrices",
    )(filter_taps, survey_mask, pairs)


def forward(window, above, own, below, r, w, left, right, copies):
    return pl.pallas_call(
        forward_kernel,
        out_shape=(struct((SCALES, XB, WIN), BF16), struct((copies, 8, PACK), F32)),
        scratch_shapes=[pltpu.VMEM((6 * XB, RAW), BF16), pltpu.VMEM((SCALES * XB, RAW), F32)],
        compiler_params=LIMIT,
        name="forward",
    )(window, above, own, below, r, w, left, right)


def shifts(g):
    return pl.pallas_call(
        shifts_kernel,
        grid=(SCALES,),
        in_specs=[per_scale((XB, WIN))],
        out_specs=per_scale((ROWS, 2 * WIDE, WIN)),
        out_shape=struct((SCALES, ROWS, 2 * WIDE, WIN), BF16),
        compiler_params=LIMIT,
        cost_estimate=cost(10_000_000, 7_000_000),
        name="shifts",
    )(g)


def backward(inverse_area, window, sums, target, weight, left, right, g, wa, ra):
    return pl.pallas_call(
        lambda *refs: backward_kernel(inverse_area, *refs),
        out_shape=(struct((PAIRS, ENTRIES), F32),) + (struct((XB, OWN), F32),) * 3,
        scratch_shapes=[pltpu.VMEM((SCALES * XB, OWN), BF16), pltpu.VMEM((SCALES * XB, OWN), BF16)],
        compiler_params=LIMIT,
        name="backward",
    )(window, sums, target, weight, left, right, g, wa, ra)


def per_device(lensing_maps, filter_taps, survey_mask, bin_pairs, target_corr, pair_weight):
    strip = lensing_maps[0]
    rows, cols = strip.shape
    bins = lax.axis_size("bin")
    sky = lax.axis_size("sky")
    pairs = bin_pairs.shape[0]
    inverse_area = 1.0 / (rows * sky * cols)
    down_perm = [(i, i + 1) for i in range(sky - 1)]
    up_perm = [(i + 1, i) for i in range(sky - 1)]

    def padded(v):
        return jnp.pad(v.reshape(pairs, ENTRIES), ((0, PAIRS - pairs), (0, 0)))

    windows = pl.pallas_call(
        windows_kernel,
        out_shape=struct((XB, RAW), BF16),
        name="windows",
    )(strip)
    own = lax.all_to_all(windows, "bin", 0, 0, tiled=True)
    r, w, wa, ra, window, left, right = matrices(filter_taps, survey_mask, bin_pairs)
    above = lax.ppermute(own, "sky", down_perm)
    below = lax.ppermute(own, "sky", up_perm)
    g, partial = forward(window, above, own, below, r, w, left, right, sky)
    moved = shifts(g)
    partial = lax.all_to_all(partial, "sky", 0, 0, tiled=True)
    partial = jnp.broadcast_to(jnp.sum(partial, axis=0)[None], (bins,) + partial.shape[1:])
    partial = lax.all_to_all(partial, "bin", 0, 0, tiled=True)
    corr, up, mid, down = backward(
        inverse_area, window, partial, padded(target_corr), padded(pair_weight),
        left, right, moved, wa, ra,
    )
    from_below = lax.ppermute(up, "sky", up_perm)
    from_above = lax.ppermute(down, "sky", down_perm)
    tile_grad = mid + from_below + from_above
    back = lax.all_to_all(tile_grad, "bin", 0, 0, tiled=True)
    map_grad = jnp.transpose(back.reshape(bins, rows, OWN), (1, 0, 2)).reshape(1, rows, cols)
    return (corr[:pairs].reshape(target_corr.shape), map_grad)


def solution(mesh):
    placed = (P("bin", "sky", None), P(), P("sky", None), P(), P(), P())
    return jax.shard_map(
        per_device,
        mesh=mesh,
        in_specs=placed,
        out_specs=(P(), P("bin", "sky", None)),
        check_vma=False,
    )
```

```python
import jax
import jax.numpy as jnp
from jax import lax
from jax.experimental import pallas as pl
from jax.experimental.pallas import tpu as pltpu
from jax.sharding import PartitionSpec as P

F32 = jnp.float32
BF16 = jnp.bfloat16
HIGH = lax.Precision.HIGHEST

BINS = 16
SCALES = 5
TAPS = 17
LAGS = 4
ROWS = 8
OWN = 512
LANE = 128
EDGE = 64
WIN = OWN + 2 * EDGE
XB = ROWS * BINS
WIDE = LAGS * BINS
TABLE = SCALES * WIDE
ENTRIES = SCALES * LAGS
PAIRS = 144
GROUPS = PAIRS // 8
PACK = 384


def full(shape):
    return pl.BlockSpec(shape, lambda *_: (0,) * len(shape))


def per_scale(shape):
    return pl.BlockSpec((1,) + shape, lambda s: (s,) + (0,) * len(shape))


SMEM = pl.BlockSpec(memory_space=pltpu.SMEM)


def split2(v):
    hi = v.astype(BF16)
    return hi, (v - hi.astype(F32)).astype(BF16)


def iota(shape, dim):
    return lax.broadcasted_iota(jnp.int32, shape, dim)


def windows_kernel(x_ref, out_ref):
    x = pltpu.roll(x_ref[...].astype(F32), EDGE, 1)
    count = x.shape[1] // OWN
    left = iota((ROWS, LANE), 1) < EDGE
    head = jnp.where(left, 0.0, x[:, :LANE])
    tail = jnp.where(left, x[:, :LANE], 0.0)

    def window(b):
        if b == 0:
            return jnp.concatenate([head, x[:, LANE:WIN]], axis=1)
        if b == count - 1:
            return jnp.concatenate([x[:, b * OWN :], tail], axis=1)
        return x[:, b * OWN : b * OWN + WIN]

    for p in range(count // 2):
        pair = jnp.concatenate([window(2 * p), window(2 * p + 1)], axis=0)
        out_ref[2 * ROWS * p : 2 * ROWS * (p + 1), :] = pair.astype(BF16)


def matrices_kernel(
    taps_ref, mask_ref, pairs_ref,
    row_ref, w_ref, wh_ref, wa_ref, row_adj_ref, window_ref, left_ref, right_ref,
):
    mask = jnp.broadcast_to(window_mask(mask_ref), (8, WIN))
    window_ref[0:8, :] = mask
    window_ref[8:16, :] = pltpu.roll(mask, WIN - EDGE, 1)
    for c, out_ref in enumerate((left_ref, right_ref)):
        bins = iota(out_ref.shape, 1) % BINS
        out_ref[...] = (pairs_ref[:, c : c + 1] == bins).astype(F32).astype(BF16)

    lane = iota((8, LANE), 1)
    n = iota((2 * LANE, LANE), 0)
    o = iota((2 * LANE, LANE), 1)
    k = o + 72 - n
    middle = (k >= 0) & (k < TAPS)
    k = jnp.where((o < EDGE) == (n >= LANE), jnp.where(o < EDGE, o + 200, o - 56) - n, -1)
    ends = (k >= 0) & (k < TAPS)

    def toeplitz(base, shift, valid):
        wide = jnp.broadcast_to(base[0:1], (2 * LANE, LANE))
        return jnp.where(valid, pltpu.roll(wide, shift, 1, stride=1, stride_axis=0), 0.0).astype(BF16)

    q = iota((ROWS, 3 * XB), 0)
    m = iota((ROWS, 3 * XB), 1)
    row_tap = m % ROWS - q + ROWS * (m // XB)
    q = iota((3 * ROWS, XB), 0)
    m = iota((3 * ROWS, XB), 1)
    row_adj_tap = q - m // BINS

    def one(s, carry):
        base = jnp.zeros((8, LANE), F32)
        flipped = jnp.zeros((8, LANE), F32)
        rows = jnp.zeros(row_tap.shape, F32)
        rows_adj = jnp.zeros(row_adj_tap.shape, F32)
        for a in range(TAPS):
            tap = taps_ref[s, a]
            base = jnp.where(lane == a, tap, base)
            flipped = jnp.where(lane == TAPS - 1 - a, tap, flipped)
            rows = jnp.where(row_tap == a, tap, rows)
            rows_adj = jnp.where(row_adj_tap == a, tap, rows_adj)
        for i in range(2):
            if i:
                base, flipped, rows, rows_adj = (
                    v - v.astype(BF16).astype(F32) for v in (base, flipped, rows, rows_adj)
                )
            base_i, flipped_i, rows_i, rows_adj_i = (
                v.astype(BF16).astype(F32) for v in (base, flipped, rows, rows_adj)
            )
            at = slice(LANE * i, LANE * (i + 1))
            w_ref[s, :, at] = toeplitz(flipped_i, LANE - 72, middle)
            wh_ref[s, :, at] = toeplitz(flipped_i, 56, ends)
            wa_ref[s, :, at] = toeplitz(base_i, LANE - 72, middle)
            row_ref[i, s] = rows_i
            row_adj_ref[i, s] = rows_adj_i
        return carry

    lax.fori_loop(0, SCALES, one, 0)


def window_mask(mask_ref):
    b = lax.axis_index("bin")
    tiles = mask_ref.shape[1]
    lane = iota((1, LANE), 1)

    def tile(t):
        value = mask_ref[0, jnp.clip(t, 0, tiles - 1)]
        return jnp.where((t >= 0) & (t < tiles), value, 0)

    first = b * (OWN // LANE)
    parts = [
        jnp.where(lane < EDGE, tile(first + f - 1), tile(first + f)) for f in range(WIN // LANE)
    ]
    return jnp.concatenate(parts, axis=1)


def banded(slabs, w):
    count = len(slabs)
    halves = [split2(slab) for slab in slabs]
    stacked = jnp.concatenate([h[i] for i in range(2) for h in halves], axis=0)
    d = jnp.dot(stacked, w, preferred_element_type=F32)
    d = d[:, :LANE] + d[:, LANE:]
    return [d[XB * f : XB * (f + 1)] + d[XB * (count + f) : XB * (count + f + 1)] for f in range(count)]


def spread_matrix():
    return (iota((ENTRIES, TABLE), 1) // BINS == iota((ENTRIES, TABLE), 0)).astype(F32).astype(BF16)


def forward_kernel(
    window_ref, up_ref, own_ref, down_ref, row_ref, w_ref, wh_ref, left_ref, right_ref,
    g_ref, out_ref, raw_ref, r_ref, pass_ref,
):

    for i, ref in enumerate((up_ref, own_ref, down_ref) * 2):
        raw_ref[XB * i : XB * (i + 1), :] = ref[...]
    own_bin = iota((BINS, 3 * XB), 0) == (iota((BINS, 3 * XB), 1) % XB) // ROWS
    for s in range(SCALES):
        for x in range(ROWS):
            for i in range(2):
                block = jnp.where(own_bin, row_ref[i, s, x : x + 1, :], 0.0).astype(BF16)
                at = XB * s + BINS * x
                r_ref[at : at + BINS, 3 * XB * i : 3 * XB * (i + 1)] = block
    pass_ref[...] = jnp.dot(r_ref[...], raw_ref[...], preferred_element_type=F32)
    mask = window_ref[8:9, :] != 0
    slab = iota((BINS, ROWS * WIDE), 1) // WIDE
    parts = []
    for s in range(SCALES):
        rows = pass_ref[XB * s : XB * (s + 1), :]
        tiles = banded([rows[:, LANE * f : LANE * (f + 2)] for f in range(OWN // LANE)], w_ref[s])
        tiles += banded([jnp.concatenate([rows[:, :LANE], rows[:, OWN:]], axis=1)], wh_ref[s])
        filtered = jnp.concatenate(tiles, axis=1).astype(BF16).astype(F32)
        g = jnp.where(mask, filtered, 0.0).astype(BF16)
        g_ref[s] = g
        left = g[:, :OWN]
        right = jnp.concatenate(
            [
                (pltpu.roll(g, WIN - l, 1) if l else g)[:, :OWN].reshape(ROWS, BINS, OWN)
                for l in range(LAGS)
            ],
            axis=1,
        ).reshape(ROWS * WIDE, OWN)
        cross = lax.dot_general(left, right, (((1,), (1,)), ((), ())), preferred_element_type=F32)
        total = jnp.zeros((BINS, ROWS * WIDE), F32)
        for x in range(ROWS):
            total = jnp.where(slab == x, cross[BINS * x : BINS * (x + 1)], total)
        total = sum(total[:, LANE * i : LANE * (i + 1)] for i in range(ROWS * WIDE // LANE))
        parts.append(total[:, :WIDE] + total[:, WIDE:])
    table = jnp.concatenate(parts, axis=1)
    pieces = []
    for _ in range(3):
        piece = table.astype(BF16)
        table = table - piece.astype(F32)
        chosen = jnp.dot(left_ref[:, 0:BINS], piece, preferred_element_type=F32)
        pieces.append(chosen.astype(BF16) * right_ref[...])
    entries = lax.dot_general(
        jnp.concatenate(pieces, axis=0), spread_matrix(), (((1,), (1,)), ((), ())),
        preferred_element_type=F32,
    )
    entries = entries[0:PAIRS] + (entries[PAIRS : 2 * PAIRS] + entries[2 * PAIRS :])
    packed = jnp.concatenate(
        [entries[8 * a : 8 * (a + 1)] for a in range(GROUPS)]
        + [jnp.zeros((8, PACK - GROUPS * ENTRIES), F32)],
        axis=1,
    )
    out_ref[...] = jnp.broadcast_to(packed[None], out_ref.shape)


def backward_kernel(
    inverse_area,
    window_ref, sums_ref, target_ref, weight_ref, left_ref, right_ref, wa_ref, row_adj_ref, g_ref,
    corr_ref, up_ref, own_ref, down_ref, hi_ref, lo_ref, ra_ref,
):
    same = iota((ROWS, XB), 1) % BINS
    for i in range(2):
        for s in range(SCALES):
            for d in range(3):
                part = row_adj_ref[i, s, ROWS * d : ROWS * (d + 1), :]
                for b in range(0, BINS, 2):
                    pair = [jnp.where(same == b + e, part, 0.0) for e in range(2)]
                    at = XB * d + ROWS * b
                    ra_ref[i, at : at + 2 * ROWS, XB * s : XB * (s + 1)] = jnp.concatenate(
                        pair, axis=0
                    ).astype(BF16)
    packed = sums_ref[0]
    for i in range(1, sums_ref.shape[0]):
        packed = packed + sums_ref[i]
    corr = inverse_area * jnp.concatenate(
        [packed[:, ENTRIES * a : ENTRIES * (a + 1)] for a in range(GROUPS)], axis=0
    )
    corr_ref[...] = corr
    grad = weight_ref[...] * (corr - target_ref[...])
    spread = spread_matrix()
    halves = []
    for piece in split2(grad):
        wide = jnp.dot(piece, spread, preferred_element_type=F32).astype(BF16)
        both = []
        for one, other in ((left_ref, right_ref), (right_ref, left_ref)):
            both.append(
                lax.dot_general(
                    one[:, 0:BINS], wide * other[...], (((0,), (0,)), ((), ())),
                    preferred_element_type=F32,
                )
            )
        halves.append(both)

    mask = window_ref[0:1, :] != 0
    for s in range(SCALES):
        at = slice(WIDE * s, WIDE * (s + 1))
        mix = jnp.concatenate(
            [jnp.concatenate([ahead[:, at], behind[:, at]], axis=1) for ahead, behind in halves],
            axis=0,
        )
        zero = jnp.zeros_like(mix)
        mix = jnp.concatenate(
            [jnp.concatenate([mix, zero], axis=1), jnp.concatenate([zero, mix], axis=1)], axis=0
        ).astype(BF16)
        rows = []
        g = g_ref[s]
        ahead = [pltpu.roll(g, EDGE - l, 1) for l in range(LAGS)]
        behind = ahead[:1] + [pltpu.roll(g, EDGE + l, 1) for l in range(1, LAGS)]
        for x in range(0, ROWS, 2):
            maps = jnp.concatenate(
                [v[BINS * y : BINS * (y + 1)] for y in (x, x + 1) for v in ahead + behind], axis=0
            )
            d = jnp.dot(mix, maps, preferred_element_type=F32)
            for i in (0, 2 * BINS):
                rows.append(jnp.where(mask, d[i : i + BINS] + d[i + BINS : i + 2 * BINS], 0.0))
        rows = jnp.concatenate(rows, axis=0)
        tiles = banded([rows[:, LANE * c : LANE * (c + 2)] for c in range(OWN // LANE)], wa_ref[s])
        for c, tile in enumerate(tiles):
            hi, lo = split2(tile)
            hi_ref[XB * s : XB * (s + 1), LANE * c : LANE * (c + 1)] = hi
            lo_ref[XB * s : XB * (s + 1), LANE * c : LANE * (c + 1)] = lo
    for i, ref in enumerate((up_ref, own_ref, down_ref)):
        at = slice(XB * i, XB * (i + 1))
        ref[...] = (
            jnp.dot(ra_ref[0, at, :], hi_ref[...], preferred_element_type=F32)
            + jnp.dot(ra_ref[0, at, :], lo_ref[...], preferred_element_type=F32)
            + jnp.dot(ra_ref[1, at, :], hi_ref[...], preferred_element_type=F32)
        )


def struct(shape, dtype):
    return jax.ShapeDtypeStruct(shape, dtype)


def limit(mib):
    return pltpu.CompilerParams(vmem_limit_bytes=mib * 1024 * 1024)


def cost(flops, moved):
    return pl.CostEstimate(flops=flops, bytes_accessed=moved, transcendentals=0)


def matrices(filter_taps, survey_mask, bin_pairs):
    pairs = jnp.pad(bin_pairs, ((0, PAIRS - bin_pairs.shape[0]), (0, 0)), constant_values=-1)
    column = struct((SCALES, 2 * LANE, 2 * LANE), BF16)
    return pl.pallas_call(
        matrices_kernel,
        in_specs=[SMEM, SMEM, VMEM],
        out_shape=(
            struct((2, SCALES, ROWS, 3 * XB), F32),
            column,
            column,
            column,
            struct((2, SCALES, 3 * ROWS, XB), F32),
            struct((16, WIN), jnp.int32),
            struct((PAIRS, TABLE), BF16),
            struct((PAIRS, TABLE), BF16),
        ),
        compiler_params=limit(32),
        cost_estimate=cost(20_000_000, 4_000_000),
        name="matrices",
    )(filter_taps, survey_mask, pairs)


VMEM = pl.BlockSpec(memory_space=pltpu.VMEM)


def forward(window, above, own, below, row, w, wh, left, right, copies):
    return pl.pallas_call(
        forward_kernel,
        out_shape=(struct((SCALES, XB, WIN), BF16), struct((copies, 8, PACK), F32)),
        scratch_shapes=[
            pltpu.VMEM((6 * XB, WIN), BF16),
            pltpu.VMEM((SCALES * XB, 6 * XB), BF16),
            pltpu.VMEM((SCALES * XB, WIN), F32),
        ],
        compiler_params=limit(32),
        name="forward",
    )(window, above, own, below, row, w, wh, left, right)


def backward(inverse_area, window, sums, target, weight, left, right, wa, row_adj, g):
    return pl.pallas_call(
        lambda *refs: backward_kernel(inverse_area, *refs),
        out_shape=(struct((PAIRS, ENTRIES), F32),) + (struct((XB, OWN), F32),) * 3,
        scratch_shapes=[
            pltpu.VMEM((SCALES * XB, OWN), BF16),
            pltpu.VMEM((SCALES * XB, OWN), BF16),
            pltpu.VMEM((2, 3 * XB, SCALES * XB), BF16),
        ],
        compiler_params=limit(32),
        name="backward",
    )(window, sums, target, weight, left, right, wa, row_adj, g)


def per_device(lensing_maps, filter_taps, survey_mask, bin_pairs, target_corr, pair_weight):
    strip = lensing_maps[0]
    rows, cols = strip.shape
    bins = lax.axis_size("bin")
    sky = lax.axis_size("sky")
    pairs = bin_pairs.shape[0]
    inverse_area = 1.0 / (rows * sky * cols)
    down_perm = [(i, i + 1) for i in range(sky - 1)]
    up_perm = [(i + 1, i) for i in range(sky - 1)]

    def padded(v):
        return jnp.pad(v.reshape(pairs, ENTRIES), ((0, PAIRS - pairs), (0, 0)))

    windows = pl.pallas_call(
        windows_kernel,
        out_shape=struct((XB, WIN), BF16),
        compiler_params=limit(8),
        name="windows",
    )(strip)
    own = lax.all_to_all(windows, "bin", 0, 0, tiled=True)
    made = matrices(filter_taps, survey_mask, bin_pairs)
    own, (row, w, wh, wa, row_adj, window, left, right) = lax.optimization_barrier((own, made))
    above = lax.ppermute(own, "sky", down_perm)
    below = lax.ppermute(own, "sky", up_perm)
    g, partial = forward(window, above, own, below, row, w, wh, left, right, sky)
    partial = lax.all_to_all(partial, "sky", 0, 0, tiled=True)
    partial = jnp.broadcast_to(jnp.sum(partial, axis=0)[None], (bins,) + partial.shape[1:])
    partial = lax.all_to_all(partial, "bin", 0, 0, tiled=True)
    corr, up, mid, down = backward(
        inverse_area, window, partial, padded(target_corr), padded(pair_weight),
        left, right, wa, row_adj, g,
    )
    from_below = lax.ppermute(up, "sky", up_perm)
    from_above = lax.ppermute(down, "sky", down_perm)
    tile_grad = mid + from_below + from_above
    back = lax.all_to_all(tile_grad, "bin", 0, 0, tiled=True)
    map_grad = jnp.transpose(back.reshape(bins, rows, OWN), (1, 0, 2)).reshape(1, rows, cols)
    return (corr[:pairs].reshape(target_corr.shape), map_grad)


def solution(mesh):
    placed = (P("bin", "sky", None), P(), P("sky", None), P(), P(), P())
    return jax.shard_map(
        per_device,
        mesh=mesh,
        in_specs=placed,
        out_specs=(P(), P("bin", "sky", None)),
        check_vma=False,
    )
```

```python
import jax
import jax.numpy as jnp
from jax import lax
from jax.experimental import pallas as pl
from jax.experimental.pallas import tpu as pltpu
from jax.sharding import PartitionSpec as P

F32 = jnp.float32
BF16 = jnp.bfloat16
HIGH = lax.Precision.HIGHEST

BINS = 16
SCALES = 5
TAPS = 17
LAGS = 4
ROWS = 8
OWN = 512
LANE = 128
EDGE = 64
WIN = OWN + 2 * EDGE
XB = ROWS * BINS
WIDE = LAGS * BINS
TABLE = SCALES * WIDE
ENTRIES = SCALES * LAGS
PAIRS = 144
GROUPS = PAIRS // 8
PACK = 384


def full(shape):
    return pl.BlockSpec(shape, lambda *_: (0,) * len(shape))


def per_scale(shape):
    return pl.BlockSpec((1,) + shape, lambda s: (s,) + (0,) * len(shape))


SMEM = pl.BlockSpec(memory_space=pltpu.SMEM)


def split2(v):
    hi = v.astype(BF16)
    return hi, (v - hi.astype(F32)).astype(BF16)


def iota(shape, dim):
    return lax.broadcasted_iota(jnp.int32, shape, dim)


def windows_kernel(x_ref, mask_ref, out_ref):
    tiles = mask_ref.shape[1]
    tiles = jnp.concatenate([mask_ref[...].astype(F32), jnp.zeros((1, LANE - tiles), F32)], axis=1)
    tiles = jnp.broadcast_to(tiles, (ROWS, LANE))
    corner = (iota((ROWS, LANE), 0) == 0) & (iota((ROWS, LANE), 1) <= WIN // LANE)
    x = pltpu.roll(x_ref[...].astype(F32), EDGE, 1)
    count = x.shape[1] // OWN
    left = iota((ROWS, LANE), 1) < EDGE
    head = jnp.where(left, 0.0, x[:, :LANE])
    tail = jnp.where(left, x[:, :LANE], 0.0)

    def window(b):
        first = head if b == 0 else x[:, b * OWN : b * OWN + LANE]
        first = jnp.where(corner, pltpu.roll(tiles, (1 - b * (OWN // LANE)) % LANE, 1), first)
        if b == count - 1:
            return jnp.concatenate([first, x[:, b * OWN + LANE :], tail], axis=1)
        return jnp.concatenate([first, x[:, b * OWN + LANE : b * OWN + WIN]], axis=1)

    for p in range(count // 2):
        pair = jnp.concatenate([window(2 * p), window(2 * p + 1)], axis=0)
        out_ref[2 * ROWS * p : 2 * ROWS * (p + 1), :] = pair.astype(BF16)


def matrices_kernel(
    taps_ref, pairs_ref, row_ref, w_ref, wh_ref, wa_ref, left_ref, right_ref, w_far, wh_far, sem,
):
    for c, out_ref in enumerate((left_ref, right_ref)):
        bins = iota(out_ref.shape, 1) % BINS
        out_ref[...] = (pairs_ref[:, c : c + 1] == bins).astype(F32).astype(BF16)

    lane = iota((8, LANE), 1)
    n = iota((2 * LANE, LANE), 0)
    o = iota((2 * LANE, LANE), 1)
    k = o + 72 - n
    middle = (k >= 0) & (k < TAPS)
    k = jnp.where((o < EDGE) == (n >= LANE), jnp.where(o < EDGE, o + 200, o - 56) - n, -1)
    ends = (k >= 0) & (k < TAPS)

    def toeplitz(base, shift, valid):
        wide = jnp.broadcast_to(base[0:1], (2 * LANE, LANE))
        return jnp.where(valid, pltpu.roll(wide, shift, 1, stride=1, stride_axis=0), 0.0).astype(BF16)

    q = iota((ROWS, 3 * XB), 0)
    m = iota((ROWS, 3 * XB), 1)
    row_tap = m % ROWS - q + ROWS * (m // XB)
    def one(s, carry):
        base = jnp.zeros((8, LANE), F32)
        flipped = jnp.zeros((8, LANE), F32)
        rows = jnp.zeros(row_tap.shape, F32)
        for a in range(TAPS):
            tap = taps_ref[s, a]
            base = jnp.where(lane == a, tap, base)
            flipped = jnp.where(lane == TAPS - 1 - a, tap, flipped)
            rows = jnp.where(row_tap == a, tap, rows)
        for i in range(2):
            if i:
                base, flipped, rows = (
                    v - v.astype(BF16).astype(F32) for v in (base, flipped, rows)
                )
            base_i, flipped_i, rows_i = (v.astype(BF16).astype(F32) for v in (base, flipped, rows))
            at = slice(LANE * i, LANE * (i + 1))
            w_ref[s, :, at] = toeplitz(flipped_i, LANE - 72, middle)
            wh_ref[s, :, at] = toeplitz(flipped_i, 56, ends)
            wa_ref[s, :, at] = toeplitz(base_i, LANE - 72, middle)
            row_ref[i, s] = rows_i
        return carry

    lax.fori_loop(0, SCALES, one, 0)
    copies = [
        pltpu.make_async_copy(near, far, sem.at[i])
        for i, (near, far) in enumerate(((w_ref, w_far), (wh_ref, wh_far)))
    ]
    for copy in copies:
        copy.start()
    for copy in copies:
        copy.wait()


def banded(slabs, w):
    count = len(slabs)
    halves = [split2(slab) for slab in slabs]
    stacked = jnp.concatenate([h[i] for i in range(2) for h in halves], axis=0)
    d = jnp.dot(stacked, w, preferred_element_type=F32)
    d = d[:, :LANE] + d[:, LANE:]
    return [d[XB * f : XB * (f + 1)] + d[XB * (count + f) : XB * (count + f + 1)] for f in range(count)]


def spread_matrix():
    return (iota((ENTRIES, TABLE), 1) // BINS == iota((ENTRIES, TABLE), 0)).astype(F32).astype(BF16)


def strip_mask(raw_ref):
    tiles = raw_ref[0:BINS, 0:LANE].astype(F32)[0:1]
    left = iota((1, LANE), 1) < EDGE
    return jnp.concatenate(
        [jnp.where(left, tiles[:, f : f + 1], tiles[:, f + 1 : f + 2]) for f in range(WIN // LANE)],
        axis=1,
    )


def filter_strip(strips, row_ref, w_ref, wh_ref, g_ref, raw_ref, r_ref, pass_ref, arrive=()):
    for copy in arrive:
        copy.start()
    for i, ref in enumerate(strips * 2):
        raw_ref[XB * i : XB * (i + 1), :] = ref[...]
    own_bin = iota((BINS, 3 * XB), 0) == (iota((BINS, 3 * XB), 1) % XB) // ROWS
    for s in range(SCALES):
        for x in range(ROWS):
            for i in range(2):
                block = jnp.where(own_bin, row_ref[i, s, x : x + 1, :], 0.0).astype(BF16)
                at = XB * s + BINS * x
                r_ref[at : at + BINS, 3 * XB * i : 3 * XB * (i + 1)] = block
    pass_ref[...] = jnp.dot(r_ref[...], raw_ref[...], preferred_element_type=F32)
    mask = jnp.broadcast_to(strip_mask(strips[1]), (BINS, WIN))
    g_ref[SCALES * XB :, :] = mask.astype(BF16)
    mask = pltpu.roll(mask, WIN - EDGE, 1)[0:1] != 0
    for copy in arrive:
        copy.wait()
    for s in range(SCALES):
        rows = pass_ref[XB * s : XB * (s + 1), :]
        tiles = banded([rows[:, LANE * f : LANE * (f + 2)] for f in range(OWN // LANE)], w_ref[s])
        tiles += banded([jnp.concatenate([rows[:, :LANE], rows[:, OWN:]], axis=1)], wh_ref[s])
        filtered = jnp.concatenate(tiles, axis=1).astype(BF16).astype(F32)
        g = jnp.where(mask, filtered, 0.0).astype(BF16)
        g_ref[XB * s : XB * (s + 1), :] = g
        yield g


def beside_kernel(
    first_ref, second_ref, third_ref, row_ref, w_far, wh_far, g_far,
    raw_ref, r_ref, pass_ref, w_ref, wh_ref, g_ref, sem,
):
    strips = (first_ref, second_ref, third_ref)
    arrive = [
        pltpu.make_async_copy(w_far, w_ref, sem.at[0]),
        pltpu.make_async_copy(wh_far, wh_ref, sem.at[1]),
    ]
    for _ in filter_strip(strips, row_ref, w_ref, wh_ref, g_ref, raw_ref, r_ref, pass_ref, arrive):
        pass
    leave = pltpu.make_async_copy(g_ref, g_far, sem.at[2])
    leave.start()
    leave.wait()


def forward_kernel(
    up_ref, own_ref, down_ref, row_ref, w_ref, wh_ref, left_ref, right_ref,
    g_ref, out_ref, raw_ref, r_ref, pass_ref,
):
    slab = iota((BINS, ROWS * WIDE), 1) // WIDE
    parts = []
    strips = (up_ref, own_ref, down_ref)
    for g in filter_strip(strips, row_ref, w_ref, wh_ref, g_ref, raw_ref, r_ref, pass_ref):
        left = g[:, :OWN]
        right = jnp.concatenate(
            [
                (pltpu.roll(g, WIN - l, 1) if l else g)[:, :OWN].reshape(ROWS, BINS, OWN)
                for l in range(LAGS)
            ],
            axis=1,
        ).reshape(ROWS * WIDE, OWN)
        cross = lax.dot_general(left, right, (((1,), (1,)), ((), ())), preferred_element_type=F32)
        total = jnp.zeros((BINS, ROWS * WIDE), F32)
        for x in range(ROWS):
            total = jnp.where(slab == x, cross[BINS * x : BINS * (x + 1)], total)
        total = sum(total[:, LANE * i : LANE * (i + 1)] for i in range(ROWS * WIDE // LANE))
        parts.append(total[:, :WIDE] + total[:, WIDE:])
    table = jnp.concatenate(parts, axis=1)
    pieces = []
    for _ in range(3):
        piece = table.astype(BF16)
        table = table - piece.astype(F32)
        chosen = jnp.dot(left_ref[:, 0:BINS], piece, preferred_element_type=F32)
        pieces.append(chosen.astype(BF16) * right_ref[...])
    entries = lax.dot_general(
        jnp.concatenate(pieces, axis=0), spread_matrix(), (((1,), (1,)), ((), ())),
        preferred_element_type=F32,
    )
    entries = entries[0:PAIRS] + (entries[PAIRS : 2 * PAIRS] + entries[2 * PAIRS :])
    packed = jnp.concatenate(
        [entries[8 * a : 8 * (a + 1)] for a in range(GROUPS)]
        + [jnp.zeros((8, PACK - GROUPS * ENTRIES), F32)],
        axis=1,
    )
    out_ref[...] = jnp.broadcast_to(packed[None], out_ref.shape)


def backward_kernel(
    inverse_area,
    taps_ref, sums_ref, target_ref, weight_ref, left_ref, right_ref, wa_ref, own_ref, up_far, down_far,
    corr_ref, out_ref, grad_ref, up_ref, down_ref, sem,
):
    copies = [
        pltpu.make_async_copy(up_far, up_ref, sem.at[0]),
        pltpu.make_async_copy(down_far, down_ref, sem.at[1]),
    ]
    for copy in copies:
        copy.start()
    packed = sums_ref[0]
    for i in range(1, sums_ref.shape[0]):
        packed = packed + sums_ref[i]
    corr = inverse_area * jnp.concatenate(
        [packed[:, ENTRIES * a : ENTRIES * (a + 1)] for a in range(GROUPS)], axis=0
    )
    corr_ref[...] = corr
    grad = weight_ref[...] * (corr - target_ref[...])
    spread = spread_matrix()
    halves = []
    for piece in split2(grad):
        wide = jnp.dot(piece, spread, preferred_element_type=F32).astype(BF16)
        both = []
        for one, other in ((left_ref, right_ref), (right_ref, left_ref)):
            both.append(
                lax.dot_general(
                    one[:, 0:BINS], wide * other[...], (((0,), (0,)), ((), ())),
                    preferred_element_type=F32,
                )
            )
        halves.append(both)

    def mask_of(ref):
        return ref[SCALES * XB :, :].astype(F32) != 0

    masks = [mask_of(own_ref)]
    totals = [jnp.zeros((XB, LANE), F32)] * (OWN // LANE)
    for s in range(SCALES):
        at = slice(WIDE * s, WIDE * (s + 1))
        mix = jnp.concatenate(
            [jnp.concatenate([ahead[:, at], behind[:, at]], axis=1) for ahead, behind in halves],
            axis=0,
        )
        zero = jnp.zeros_like(mix)
        mix = jnp.concatenate(
            [jnp.concatenate([mix, zero], axis=1), jnp.concatenate([zero, mix], axis=1)], axis=0
        ).astype(BF16)
        for n, (k, ref) in enumerate(((1, own_ref), (0, up_ref), (2, down_ref))):
            if s == 0 and n == 1:
                for copy in copies:
                    copy.wait()
                masks += [mask_of(up_ref), mask_of(down_ref)]
            mask = masks[n]
            g = ref[XB * s : XB * (s + 1), :]
            ahead = [pltpu.roll(g, EDGE - l, 1) for l in range(LAGS)]
            behind = ahead[:1] + [pltpu.roll(g, EDGE + l, 1) for l in range(1, LAGS)]
            for x in range(0, ROWS, 2):
                maps = jnp.concatenate(
                    [v[BINS * y : BINS * (y + 1)] for y in (x, x + 1) for v in ahead + behind], axis=0
                )
                d = jnp.dot(mix, maps, preferred_element_type=F32)
                for i in range(2):
                    v = d[2 * BINS * i : 2 * BINS * (i + 1)]
                    grad_ref[s % 2, ROWS * k + x + i] = jnp.where(mask, v[:BINS] + v[BINS:], 0.0)
        rows = []
        for x in range(ROWS):
            acc = taps_ref[s, TAPS - 1] * grad_ref[s % 2, x]
            for a in range(1, TAPS):
                acc = acc + taps_ref[s, TAPS - 1 - a] * grad_ref[s % 2, x + a]
            rows.append(acc)
        rows = jnp.concatenate(rows, axis=0)
        tiles = banded([rows[:, LANE * c : LANE * (c + 2)] for c in range(OWN // LANE)], wa_ref[s])
        totals = [total + tile for total, tile in zip(totals, tiles)]
    for c, total in enumerate(totals):
        for x in range(ROWS):
            at = pl.ds(ROWS * c + x, BINS, stride=ROWS * OWN // LANE)
            out_ref[at, :] = total[BINS * x : BINS * (x + 1)]


def struct(shape, dtype):
    return jax.ShapeDtypeStruct(shape, dtype)


VMEM = pl.BlockSpec(memory_space=pltpu.VMEM)
HBM = pl.BlockSpec(memory_space=pltpu.HBM)
COLUMN = (SCALES, 2 * LANE, 2 * LANE)
MAPS = (SCALES * XB + BINS, WIN)


def far(v):
    return pltpu.with_memory_space_constraint(v, pltpu.HBM)


def limit(mib):
    return pltpu.CompilerParams(vmem_limit_bytes=mib * 1024 * 1024)


def cost(flops, moved):
    return pl.CostEstimate(flops=flops, bytes_accessed=moved, transcendentals=0)


def matrices(filter_taps, bin_pairs):
    pairs = jnp.pad(bin_pairs, ((0, PAIRS - bin_pairs.shape[0]), (0, 0)), constant_values=-1)
    column = struct(COLUMN, BF16)
    return pl.pallas_call(
        matrices_kernel,
        in_specs=[SMEM, VMEM],
        out_shape=(
            struct((2, SCALES, ROWS, 3 * XB), F32),
            column,
            column,
            column,
            struct((PAIRS, TABLE), BF16),
            struct((PAIRS, TABLE), BF16),
            pltpu.HBM(COLUMN, BF16),
            pltpu.HBM(COLUMN, BF16),
        ),
        out_specs=[VMEM] * 6 + [HBM] * 2,
        scratch_shapes=[pltpu.SemaphoreType.DMA((2,))],
        compiler_params=limit(32),
        cost_estimate=cost(20_000_000, 4_000_000),
        name="matrices",
    )(filter_taps, pairs)


def scratch():
    return [
        pltpu.VMEM((6 * XB, WIN), BF16),
        pltpu.VMEM((SCALES * XB, 6 * XB), BF16),
        pltpu.VMEM((SCALES * XB, WIN), F32),
    ]


def forward(strips, row, w, wh, left, right, copies):
    return pl.pallas_call(
        forward_kernel,
        out_shape=(struct(MAPS, BF16), struct((copies, 8, PACK), F32)),
        scratch_shapes=scratch(),
        compiler_params=limit(32),
        name="forward",
    )(*strips, row, w, wh, left, right)


def beside(strips, row, w, wh):
    return pl.pallas_call(
        beside_kernel,
        in_specs=[VMEM] * 4 + [HBM] * 2,
        out_specs=HBM,
        out_shape=pltpu.HBM(MAPS, BF16),
        scratch_shapes=scratch()
        + [
            pltpu.VMEM(COLUMN, BF16),
            pltpu.VMEM(COLUMN, BF16),
            pltpu.VMEM(MAPS, BF16),
            pltpu.SemaphoreType.DMA((3,)),
        ],
        compiler_params=limit(32),
        cost_estimate=cost(2_000_000_000, 8_000_000),
        name="beside",
    )(*strips, row, far(w), far(wh))


def backward(inverse_area, taps, sums, target, weight, left, right, wa, above, own, below):
    return pl.pallas_call(
        lambda *refs: backward_kernel(inverse_area, *refs),
        in_specs=[SMEM] + [VMEM] * 7 + [HBM] * 2,
        out_shape=(struct((PAIRS, ENTRIES), F32), struct((XB * OWN // LANE, LANE), F32)),
        scratch_shapes=[
            pltpu.VMEM((2, 3 * ROWS, BINS, WIN), F32),
            pltpu.VMEM(MAPS, BF16),
            pltpu.VMEM(MAPS, BF16),
            pltpu.SemaphoreType.DMA((2,)),
        ],
        compiler_params=limit(32),
        name="backward",
    )(taps, sums, target, weight, left, right, wa, own, far(above), far(below))


def per_device(lensing_maps, filter_taps, survey_mask, bin_pairs, target_corr, pair_weight):
    strip = lensing_maps[0]
    rows, cols = strip.shape
    bins = lax.axis_size("bin")
    sky = lax.axis_size("sky")
    pairs = bin_pairs.shape[0]
    inverse_area = 1.0 / (rows * sky * cols)
    down_perm = [(i, i + 1) for i in range(sky - 1)]
    up_perm = [(i + 1, i) for i in range(sky - 1)]

    def padded(v):
        return jnp.pad(v.reshape(pairs, ENTRIES), ((0, PAIRS - pairs), (0, 0)))

    windows = pl.pallas_call(
        windows_kernel,
        out_shape=struct((XB, WIN), BF16),
        compiler_params=limit(8),
        name="windows",
    )(strip, survey_mask)
    own = lax.all_to_all(windows, "bin", 0, 0, tiled=True)
    made = matrices(filter_taps, bin_pairs)
    own, (row, w, wh, wa, left, right, w_far, wh_far) = lax.optimization_barrier((own, made))
    above = lax.ppermute(own, "sky", down_perm)
    below = lax.ppermute(own, "sky", up_perm)
    above2 = lax.ppermute(own, "sky", [(i, i + 2) for i in range(sky - 2)])
    below2 = lax.ppermute(own, "sky", [(i + 2, i) for i in range(sky - 2)])
    g, partial = forward((above, own, below), row, w, wh, left, right, sky)
    g_above = beside((above2, above, own), row, w_far, wh_far)
    g_below = beside((own, below, below2), row, w_far, wh_far)
    partial = lax.all_to_all(partial, "sky", 0, 0, tiled=True)
    partial = jnp.broadcast_to(jnp.sum(partial, axis=0)[None], (bins,) + partial.shape[1:])
    partial = lax.all_to_all(partial, "bin", 0, 0, tiled=True)
    corr, tile_grad = backward(
        inverse_area, filter_taps, partial, padded(target_corr), padded(pair_weight),
        left, right, wa, g_above, g, g_below,
    )
    back = lax.all_to_all(tile_grad, "bin", 0, 0, tiled=True)
    map_grad = jnp.transpose(back.reshape(cols // LANE, rows, LANE), (1, 0, 2)).reshape(1, rows, cols)
    return (corr[:pairs].reshape(target_corr.shape), map_grad)


def solution(mesh):
    placed = (P("bin", "sky", None), P(), P("sky", None), P(), P(), P())
    return jax.shard_map(
        per_device,
        mesh=mesh,
        in_specs=placed,
        out_specs=(P(), P("bin", "sky", None)),
        check_vma=False,
    )
```

```python
import jax
import jax.numpy as jnp
from jax import lax
from jax.experimental import pallas as pl
from jax.experimental.pallas import tpu as pltpu
from jax.sharding import PartitionSpec as P

F32 = jnp.float32
BF16 = jnp.bfloat16
HIGH = lax.Precision.HIGHEST

BINS = 16
SCALES = 5
TAPS = 17
LAGS = 4
ROWS = 8
OWN = 512
LANE = 128
EDGE = 64
WIN = OWN + 2 * EDGE
XB = ROWS * BINS
WIDE = LAGS * BINS
TABLE = SCALES * WIDE
ENTRIES = SCALES * LAGS
PAIRS = 144
GROUPS = PAIRS // 8
PACK = 384


def full(shape):
    return pl.BlockSpec(shape, lambda *_: (0,) * len(shape))


def per_scale(shape):
    return pl.BlockSpec((1,) + shape, lambda s: (s,) + (0,) * len(shape))


SMEM = pl.BlockSpec(memory_space=pltpu.SMEM)


def split2(v):
    hi = v.astype(BF16)
    return hi, (v - hi.astype(F32)).astype(BF16)


def iota(shape, dim):
    return lax.broadcasted_iota(jnp.int32, shape, dim)


def windows_kernel(x_ref, mask_ref, out_ref):
    tiles = mask_ref.shape[1]
    tiles = jnp.concatenate([mask_ref[...].astype(F32), jnp.zeros((1, LANE - tiles), F32)], axis=1)
    tiles = jnp.broadcast_to(tiles, (ROWS, LANE))
    corner = (iota((ROWS, LANE), 0) == 0) & (iota((ROWS, LANE), 1) <= WIN // LANE)
    x = pltpu.roll(x_ref[...].astype(F32), EDGE, 1)
    count = x.shape[1] // OWN
    left = iota((ROWS, LANE), 1) < EDGE
    head = jnp.where(left, 0.0, x[:, :LANE])
    tail = jnp.where(left, x[:, :LANE], 0.0)

    def window(b):
        first = head if b == 0 else x[:, b * OWN : b * OWN + LANE]
        first = jnp.where(corner, pltpu.roll(tiles, (1 - b * (OWN // LANE)) % LANE, 1), first)
        if b == count - 1:
            return jnp.concatenate([first, x[:, b * OWN + LANE :], tail], axis=1)
        return jnp.concatenate([first, x[:, b * OWN + LANE : b * OWN + WIN]], axis=1)

    for p in range(count // 2):
        pair = jnp.concatenate([window(2 * p), window(2 * p + 1)], axis=0)
        out_ref[2 * ROWS * p : 2 * ROWS * (p + 1), :] = pair.astype(BF16)


def matrices_kernel(
    taps_ref, pairs_ref, row_ref, w_ref, wh_ref, left_ref, right_ref,
    w_far, wh_far, wa_far, wa_ref, sem,
):
    for c, out_ref in enumerate((left_ref, right_ref)):
        bins = iota(out_ref.shape, 1) % BINS
        out_ref[...] = (pairs_ref[:, c : c + 1] == bins).astype(F32).astype(BF16)

    lane = iota((8, LANE), 1)
    n = iota((2 * LANE, LANE), 0)
    o = iota((2 * LANE, LANE), 1)
    k = o + 72 - n
    middle = (k >= 0) & (k < TAPS)
    k = jnp.where((o < EDGE) == (n >= LANE), jnp.where(o < EDGE, o + 200, o - 56) - n, -1)
    ends = (k >= 0) & (k < TAPS)

    def toeplitz(base, shift, valid):
        wide = jnp.broadcast_to(base[0:1], (2 * LANE, LANE))
        return jnp.where(valid, pltpu.roll(wide, shift, 1, stride=1, stride_axis=0), 0.0).astype(BF16)

    q = iota((ROWS, 3 * XB), 0)
    m = iota((ROWS, 3 * XB), 1)
    row_tap = m % ROWS - q + ROWS * (m // XB)
    def one(s, carry):
        base = jnp.zeros((8, LANE), F32)
        flipped = jnp.zeros((8, LANE), F32)
        rows = jnp.zeros(row_tap.shape, F32)
        for a in range(TAPS):
            tap = taps_ref[s, a]
            base = jnp.where(lane == a, tap, base)
            flipped = jnp.where(lane == TAPS - 1 - a, tap, flipped)
            rows = jnp.where(row_tap == a, tap, rows)
        for i in range(2):
            if i:
                base, flipped, rows = (
                    v - v.astype(BF16).astype(F32) for v in (base, flipped, rows)
                )
            base_i, flipped_i, rows_i = (v.astype(BF16).astype(F32) for v in (base, flipped, rows))
            at = slice(LANE * i, LANE * (i + 1))
            w_ref[s, :, at] = toeplitz(flipped_i, LANE - 72, middle)
            wh_ref[s, :, at] = toeplitz(flipped_i, 56, ends)
            wa_ref[s, :, at] = toeplitz(base_i, LANE - 72, middle)
            row_ref[i, s] = rows_i
        return carry

    lax.fori_loop(0, SCALES, one, 0)
    copies = [
        pltpu.make_async_copy(near, far, sem.at[i])
        for i, (near, far) in enumerate(((w_ref, w_far), (wh_ref, wh_far), (wa_ref, wa_far)))
    ]
    for copy in copies:
        copy.start()
    for copy in copies:
        copy.wait()


def banded(slabs, w):
    count = len(slabs)
    halves = [split2(slab) for slab in slabs]
    stacked = jnp.concatenate([h[i] for i in range(2) for h in halves], axis=0)
    d = jnp.dot(stacked, w, preferred_element_type=F32)
    d = d[:, :LANE] + d[:, LANE:]
    return [d[XB * f : XB * (f + 1)] + d[XB * (count + f) : XB * (count + f + 1)] for f in range(count)]


def spread_matrix():
    return (iota((ENTRIES, TABLE), 1) // BINS == iota((ENTRIES, TABLE), 0)).astype(F32).astype(BF16)


def strip_mask(raw_ref):
    tiles = raw_ref[0:BINS, 0:LANE].astype(F32)[0:1]
    left = iota((1, LANE), 1) < EDGE
    return jnp.concatenate(
        [jnp.where(left, tiles[:, f : f + 1], tiles[:, f + 1 : f + 2]) for f in range(WIN // LANE)],
        axis=1,
    )


def filter_strip(strips, row_ref, w_ref, wh_ref, g_ref, raw_ref, r_ref, pass_ref, arrive=()):
    for copy in arrive:
        copy.start()
    for i, ref in enumerate(strips * 2):
        raw_ref[XB * i : XB * (i + 1), :] = ref[...]
    own_bin = iota((BINS, 3 * XB), 0) == (iota((BINS, 3 * XB), 1) % XB) // ROWS
    for s in range(SCALES):
        for x in range(ROWS):
            for i in range(2):
                block = jnp.where(own_bin, row_ref[i, s, x : x + 1, :], 0.0).astype(BF16)
                at = XB * s + BINS * x
                r_ref[at : at + BINS, 3 * XB * i : 3 * XB * (i + 1)] = block
    pass_ref[...] = jnp.dot(r_ref[...], raw_ref[...], preferred_element_type=F32)
    mask = jnp.broadcast_to(strip_mask(strips[1]), (BINS, WIN))
    g_ref[SCALES * XB :, :] = mask.astype(BF16)
    mask = pltpu.roll(mask, WIN - EDGE, 1)[0:1] != 0
    for copy in arrive:
        copy.wait()
    for s in range(SCALES):
        rows = pass_ref[XB * s : XB * (s + 1), :]
        tiles = banded([rows[:, LANE * f : LANE * (f + 2)] for f in range(OWN // LANE)], w_ref[s])
        tiles += banded([jnp.concatenate([rows[:, :LANE], rows[:, OWN:]], axis=1)], wh_ref[s])
        filtered = jnp.concatenate(tiles, axis=1).astype(BF16).astype(F32)
        g = jnp.where(mask, filtered, 0.0).astype(BF16)
        g_ref[XB * s : XB * (s + 1), :] = g
        yield g


def beside_kernel(
    first_ref, second_ref, third_ref, row_ref, w_far, wh_far, g_far,
    raw_ref, r_ref, pass_ref, w_ref, wh_ref, g_ref, sem,
):
    strips = (first_ref, second_ref, third_ref)
    arrive = [
        pltpu.make_async_copy(w_far, w_ref, sem.at[0]),
        pltpu.make_async_copy(wh_far, wh_ref, sem.at[1]),
    ]
    for _ in filter_strip(strips, row_ref, w_ref, wh_ref, g_ref, raw_ref, r_ref, pass_ref, arrive):
        pass
    leave = pltpu.make_async_copy(g_ref, g_far, sem.at[2])
    leave.start()
    leave.wait()


def forward_kernel(
    up_ref, own_ref, down_ref, row_ref, w_ref, wh_ref, left_ref, right_ref,
    g_ref, out_ref, raw_ref, r_ref, pass_ref,
):
    slab = iota((BINS, ROWS * WIDE), 1) // WIDE
    parts = []
    strips = (up_ref, own_ref, down_ref)
    for g in filter_strip(strips, row_ref, w_ref, wh_ref, g_ref, raw_ref, r_ref, pass_ref):
        left = g[:, :OWN]
        right = jnp.concatenate(
            [
                (pltpu.roll(g, WIN - l, 1) if l else g)[:, :OWN].reshape(ROWS, BINS, OWN)
                for l in range(LAGS)
            ],
            axis=1,
        ).reshape(ROWS * WIDE, OWN)
        cross = lax.dot_general(left, right, (((1,), (1,)), ((), ())), preferred_element_type=F32)
        total = jnp.zeros((BINS, ROWS * WIDE), F32)
        for x in range(ROWS):
            total = jnp.where(slab == x, cross[BINS * x : BINS * (x + 1)], total)
        total = sum(total[:, LANE * i : LANE * (i + 1)] for i in range(ROWS * WIDE // LANE))
        parts.append(total[:, :WIDE] + total[:, WIDE:])
    table = jnp.concatenate(parts, axis=1)
    pieces = []
    for _ in range(3):
        piece = table.astype(BF16)
        table = table - piece.astype(F32)
        chosen = jnp.dot(left_ref[:, 0:BINS], piece, preferred_element_type=F32)
        pieces.append(chosen.astype(BF16) * right_ref[...])
    entries = lax.dot_general(
        jnp.concatenate(pieces, axis=0), spread_matrix(), (((1,), (1,)), ((), ())),
        preferred_element_type=F32,
    )
    entries = entries[0:PAIRS] + (entries[PAIRS : 2 * PAIRS] + entries[2 * PAIRS :])
    packed = jnp.concatenate(
        [entries[8 * a : 8 * (a + 1)] for a in range(GROUPS)]
        + [jnp.zeros((8, PACK - GROUPS * ENTRIES), F32)],
        axis=1,
    )
    out_ref[...] = jnp.broadcast_to(packed[None], out_ref.shape)


def backward_kernel(
    inverse_area,
    taps_ref, sums_ref, target_ref, weight_ref, left_ref, right_ref, own_ref, up_far, down_far, wa_far,
    corr_ref, out_ref, grad_ref, up_ref, down_ref, wa_ref, sem,
):
    copies = [
        pltpu.make_async_copy(up_far, up_ref, sem.at[0]),
        pltpu.make_async_copy(down_far, down_ref, sem.at[1]),
        pltpu.make_async_copy(wa_far, wa_ref, sem.at[2]),
    ]
    for copy in copies:
        copy.start()
    packed = sums_ref[0]
    for i in range(1, sums_ref.shape[0]):
        packed = packed + sums_ref[i]
    corr = inverse_area * jnp.concatenate(
        [packed[:, ENTRIES * a : ENTRIES * (a + 1)] for a in range(GROUPS)], axis=0
    )
    corr_ref[...] = corr
    grad = weight_ref[...] * (corr - target_ref[...])
    spread = spread_matrix()
    halves = []
    for piece in split2(grad):
        wide = jnp.dot(piece, spread, preferred_element_type=F32).astype(BF16)
        both = []
        for one, other in ((left_ref, right_ref), (right_ref, left_ref)):
            both.append(
                lax.dot_general(
                    one[:, 0:BINS], wide * other[...], (((0,), (0,)), ((), ())),
                    preferred_element_type=F32,
                )
            )
        halves.append(both)

    def mask_of(ref):
        return ref[SCALES * XB :, :].astype(F32) != 0

    masks = [mask_of(own_ref)]
    totals = [jnp.zeros((XB, LANE), F32)] * (OWN // LANE)
    for s in range(SCALES):
        at = slice(WIDE * s, WIDE * (s + 1))
        mix = jnp.concatenate(
            [jnp.concatenate([ahead[:, at], behind[:, at]], axis=1) for ahead, behind in halves],
            axis=0,
        )
        zero = jnp.zeros_like(mix)
        mix = jnp.concatenate(
            [jnp.concatenate([mix, zero], axis=1), jnp.concatenate([zero, mix], axis=1)], axis=0
        ).astype(BF16)
        for n, (k, ref) in enumerate(((1, own_ref), (0, up_ref), (2, down_ref))):
            if s == 0 and n == 1:
                for copy in copies:
                    copy.wait()
                masks += [mask_of(up_ref), mask_of(down_ref)]
            mask = masks[n]
            g = ref[XB * s : XB * (s + 1), :]
            ahead = [pltpu.roll(g, EDGE - l, 1) for l in range(LAGS)]
            behind = ahead[:1] + [pltpu.roll(g, EDGE + l, 1) for l in range(1, LAGS)]
            for x in range(0, ROWS, 2):
                maps = jnp.concatenate(
                    [v[BINS * y : BINS * (y + 1)] for y in (x, x + 1) for v in ahead + behind], axis=0
                )
                d = jnp.dot(mix, maps, preferred_element_type=F32)
                for i in range(2):
                    v = d[2 * BINS * i : 2 * BINS * (i + 1)]
                    grad_ref[s % 2, ROWS * k + x + i] = jnp.where(mask, v[:BINS] + v[BINS:], 0.0)
        rows = []
        for x in range(ROWS):
            acc = taps_ref[s, TAPS - 1] * grad_ref[s % 2, x]
            for a in range(1, TAPS):
                acc = acc + taps_ref[s, TAPS - 1 - a] * grad_ref[s % 2, x + a]
            rows.append(acc)
        rows = jnp.concatenate(rows, axis=0)
        tiles = banded([rows[:, LANE * c : LANE * (c + 2)] for c in range(OWN // LANE)], wa_ref[s])
        totals = [total + tile for total, tile in zip(totals, tiles)]
    for c, total in enumerate(totals):
        for x in range(ROWS):
            at = pl.ds(ROWS * c + x, BINS, stride=ROWS * OWN // LANE)
            out_ref[at, :] = total[BINS * x : BINS * (x + 1)]


def struct(shape, dtype):
    return jax.ShapeDtypeStruct(shape, dtype)


VMEM = pl.BlockSpec(memory_space=pltpu.VMEM)
HBM = pl.BlockSpec(memory_space=pltpu.HBM)
COLUMN = (SCALES, 2 * LANE, 2 * LANE)
MAPS = (SCALES * XB + BINS, WIN)


def far(v):
    return pltpu.with_memory_space_constraint(v, pltpu.HBM)


def limit(mib):
    return pltpu.CompilerParams(vmem_limit_bytes=mib * 1024 * 1024)


def cost(flops, moved):
    return pl.CostEstimate(flops=flops, bytes_accessed=moved, transcendentals=0)


def matrices(filter_taps, bin_pairs):
    pairs = jnp.pad(bin_pairs, ((0, PAIRS - bin_pairs.shape[0]), (0, 0)), constant_values=-1)
    column = struct(COLUMN, BF16)
    return pl.pallas_call(
        matrices_kernel,
        in_specs=[SMEM, VMEM],
        out_shape=(
            struct((2, SCALES, ROWS, 3 * XB), F32),
            column,
            column,
            struct((PAIRS, TABLE), BF16),
            struct((PAIRS, TABLE), BF16),
            pltpu.HBM(COLUMN, BF16),
            pltpu.HBM(COLUMN, BF16),
            pltpu.HBM(COLUMN, BF16),
        ),
        out_specs=[VMEM] * 5 + [HBM] * 3,
        scratch_shapes=[pltpu.VMEM(COLUMN, BF16), pltpu.SemaphoreType.DMA((3,))],
        compiler_params=limit(32),
        cost_estimate=cost(20_000_000, 4_000_000),
        name="matrices",
    )(filter_taps, pairs)


def scratch():
    return [
        pltpu.VMEM((6 * XB, WIN), BF16),
        pltpu.VMEM((SCALES * XB, 6 * XB), BF16),
        pltpu.VMEM((SCALES * XB, WIN), F32),
    ]


def forward(strips, row, w, wh, left, right, copies):
    return pl.pallas_call(
        forward_kernel,
        out_shape=(struct(MAPS, BF16), struct((copies, 8, PACK), F32)),
        scratch_shapes=scratch(),
        compiler_params=limit(32),
        name="forward",
    )(*strips, row, w, wh, left, right)


def beside(strips, row, w, wh):
    return pl.pallas_call(
        beside_kernel,
        in_specs=[VMEM] * 4 + [HBM] * 2,
        out_specs=HBM,
        out_shape=pltpu.HBM(MAPS, BF16),
        scratch_shapes=scratch()
        + [
            pltpu.VMEM(COLUMN, BF16),
            pltpu.VMEM(COLUMN, BF16),
            pltpu.VMEM(MAPS, BF16),
            pltpu.SemaphoreType.DMA((3,)),
        ],
        compiler_params=limit(32),
        cost_estimate=cost(2_000_000_000, 8_000_000),
        name="beside",
    )(*strips, row, far(w), far(wh))


def backward(inverse_area, taps, sums, target, weight, left, right, wa, above, own, below):
    return pl.pallas_call(
        lambda *refs: backward_kernel(inverse_area, *refs),
        in_specs=[SMEM] + [VMEM] * 6 + [HBM] * 3,
        out_shape=(struct((PAIRS, ENTRIES), F32), struct((XB * OWN // LANE, LANE), F32)),
        scratch_shapes=[
            pltpu.VMEM((2, 3 * ROWS, BINS, WIN), F32),
            pltpu.VMEM(MAPS, BF16),
            pltpu.VMEM(MAPS, BF16),
            pltpu.VMEM(COLUMN, BF16),
            pltpu.SemaphoreType.DMA((3,)),
        ],
        compiler_params=limit(32),
        name="backward",
    )(taps, sums, target, weight, left, right, own, far(above), far(below), far(wa))


def per_device(lensing_maps, filter_taps, survey_mask, bin_pairs, target_corr, pair_weight):
    strip = lensing_maps[0]
    rows, cols = strip.shape
    bins = lax.axis_size("bin")
    sky = lax.axis_size("sky")
    pairs = bin_pairs.shape[0]
    inverse_area = 1.0 / (rows * sky * cols)
    down_perm = [(i, i + 1) for i in range(sky - 1)]
    up_perm = [(i + 1, i) for i in range(sky - 1)]

    def padded(v):
        return jnp.pad(v.reshape(pairs, ENTRIES), ((0, PAIRS - pairs), (0, 0)))

    windows = pl.pallas_call(
        windows_kernel,
        out_shape=struct((XB, WIN), BF16),
        compiler_params=limit(60),
        name="windows",
    )(strip, survey_mask)
    own = lax.all_to_all(windows, "bin", 0, 0, tiled=True)
    made = matrices(filter_taps, bin_pairs)
    own, (row, w, wh, left, right, w_far, wh_far, wa) = lax.optimization_barrier((own, made))
    above = lax.ppermute(own, "sky", down_perm)
    below = lax.ppermute(own, "sky", up_perm)
    above2 = lax.ppermute(own, "sky", [(i, i + 2) for i in range(sky - 2)])
    below2 = lax.ppermute(own, "sky", [(i + 2, i) for i in range(sky - 2)])
    g, partial = forward((above, own, below), row, w, wh, left, right, sky)
    g_above = beside((above2, above, own), row, w_far, wh_far)
    g_below = beside((own, below, below2), row, w_far, wh_far)
    partial = lax.all_to_all(partial, "sky", 0, 0, tiled=True)
    partial = jnp.broadcast_to(jnp.sum(partial, axis=0)[None], (bins,) + partial.shape[1:])
    partial = lax.all_to_all(partial, "bin", 0, 0, tiled=True)
    corr, tile_grad = backward(
        inverse_area, filter_taps, partial, padded(target_corr), padded(pair_weight),
        left, right, wa, g_above, g, g_below,
    )
    back = lax.all_to_all(tile_grad, "bin", 0, 0, tiled=True)
    map_grad = jnp.transpose(back.reshape(cols // LANE, rows, LANE), (1, 0, 2)).reshape(1, rows, cols)
    return (corr[:pairs].reshape(target_corr.shape), map_grad)


def solution(mesh):
    placed = (P("bin", "sky", None), P(), P("sky", None), P(), P(), P())
    return jax.shard_map(
        per_device,
        mesh=mesh,
        in_specs=placed,
        out_specs=(P(), P("bin", "sky", None)),
        check_vma=False,
    )
```

```python
import jax
import jax.numpy as jnp
from jax import lax
from jax.experimental import pallas as pl
from jax.experimental.pallas import tpu as pltpu
from jax.sharding import PartitionSpec as P

F32 = jnp.float32
BF16 = jnp.bfloat16
HIGH = lax.Precision.HIGHEST

BINS = 16
SCALES = 5
TAPS = 17
LAGS = 4
ROWS = 8
OWN = 512
LANE = 128
EDGE = 64
WIN = OWN + 2 * EDGE
XB = ROWS * BINS
WIDE = LAGS * BINS
TABLE = SCALES * WIDE
ENTRIES = SCALES * LAGS
PAIRS = 144
GROUPS = PAIRS // 8
PACK = 384


def full(shape):
    return pl.BlockSpec(shape, lambda *_: (0,) * len(shape))


def per_scale(shape):
    return pl.BlockSpec((1,) + shape, lambda s: (s,) + (0,) * len(shape))


SMEM = pl.BlockSpec(memory_space=pltpu.SMEM)


def split2(v):
    hi = v.astype(BF16)
    return hi, (v - hi.astype(F32)).astype(BF16)


def iota(shape, dim):
    return lax.broadcasted_iota(jnp.int32, shape, dim)


def windows_kernel(x_ref, mask_ref, out_ref):
    tiles = mask_ref.shape[1]
    tiles = jnp.concatenate([mask_ref[...].astype(F32), jnp.zeros((1, LANE - tiles), F32)], axis=1)
    tiles = jnp.broadcast_to(tiles, (ROWS, LANE))
    corner = (iota((ROWS, LANE), 0) == 0) & (iota((ROWS, LANE), 1) <= WIN // LANE)
    x = pltpu.roll(x_ref[...].astype(F32), EDGE, 1)
    count = x.shape[1] // OWN
    left = iota((ROWS, LANE), 1) < EDGE
    head = jnp.where(left, 0.0, x[:, :LANE])
    tail = jnp.where(left, x[:, :LANE], 0.0)

    def window(b):
        first = head if b == 0 else x[:, b * OWN : b * OWN + LANE]
        first = jnp.where(corner, pltpu.roll(tiles, (1 - b * (OWN // LANE)) % LANE, 1), first)
        if b == count - 1:
            return jnp.concatenate([first, x[:, b * OWN + LANE :], tail], axis=1)
        return jnp.concatenate([first, x[:, b * OWN + LANE : b * OWN + WIN]], axis=1)

    for p in range(count // 2):
        pair = jnp.concatenate([window(2 * p), window(2 * p + 1)], axis=0)
        out_ref[2 * ROWS * p : 2 * ROWS * (p + 1), :] = pair.astype(BF16)


def matrices_kernel(
    taps_ref, pairs_ref, row_ref, w_ref, wh_ref, left_ref, right_ref,
    w_far, wh_far, wa_far, wa_ref, sem,
):
    for c, out_ref in enumerate((left_ref, right_ref)):
        bins = iota(out_ref.shape, 1) % BINS
        out_ref[...] = (pairs_ref[:, c : c + 1] == bins).astype(F32).astype(BF16)

    lane = iota((8, LANE), 1)
    n = iota((2 * LANE, LANE), 0)
    o = iota((2 * LANE, LANE), 1)
    k = o + 72 - n
    middle = (k >= 0) & (k < TAPS)
    k = jnp.where((o < EDGE) == (n >= LANE), jnp.where(o < EDGE, o + 200, o - 56) - n, -1)
    ends = (k >= 0) & (k < TAPS)

    def toeplitz(base, shift, valid):
        wide = jnp.broadcast_to(base[0:1], (2 * LANE, LANE))
        return jnp.where(valid, pltpu.roll(wide, shift, 1, stride=1, stride_axis=0), 0.0).astype(BF16)

    q = iota((ROWS, 3 * XB), 0)
    m = iota((ROWS, 3 * XB), 1)
    row_tap = m % ROWS - q + ROWS * (m // XB)
    def one(s, carry):
        base = jnp.zeros((8, LANE), F32)
        flipped = jnp.zeros((8, LANE), F32)
        rows = jnp.zeros(row_tap.shape, F32)
        for a in range(TAPS):
            tap = taps_ref[s, a]
            base = jnp.where(lane == a, tap, base)
            flipped = jnp.where(lane == TAPS - 1 - a, tap, flipped)
            rows = jnp.where(row_tap == a, tap, rows)
        for i in range(2):
            if i:
                base, flipped, rows = (
                    v - v.astype(BF16).astype(F32) for v in (base, flipped, rows)
                )
            base_i, flipped_i, rows_i = (v.astype(BF16).astype(F32) for v in (base, flipped, rows))
            at = slice(LANE * i, LANE * (i + 1))
            w_ref[s, :, at] = toeplitz(flipped_i, LANE - 72, middle)
            wh_ref[s, :, at] = toeplitz(flipped_i, 56, ends)
            wa_ref[s, :, at] = toeplitz(base_i, LANE - 72, middle)
            row_ref[i, s] = rows_i
        return carry

    lax.fori_loop(0, SCALES, one, 0)
    copies = [
        pltpu.make_async_copy(near, far, sem.at[i])
        for i, (near, far) in enumerate(((w_ref, w_far), (wh_ref, wh_far), (wa_ref, wa_far)))
    ]
    for copy in copies:
        copy.start()
    for copy in copies:
        copy.wait()


def banded(slabs, w):
    count = len(slabs)
    halves = [split2(slab) for slab in slabs]
    stacked = jnp.concatenate([h[i] for i in range(2) for h in halves], axis=0)
    d = jnp.dot(stacked, w, preferred_element_type=F32)
    d = d[:, :LANE] + d[:, LANE:]
    return [d[XB * f : XB * (f + 1)] + d[XB * (count + f) : XB * (count + f + 1)] for f in range(count)]


def spread_matrix():
    return (iota((ENTRIES, TABLE), 1) // BINS == iota((ENTRIES, TABLE), 0)).astype(F32).astype(BF16)


def strip_mask(raw_ref):
    tiles = raw_ref[0:BINS, 0:LANE].astype(F32)[0:1]
    left = iota((1, LANE), 1) < EDGE
    return jnp.concatenate(
        [jnp.where(left, tiles[:, f : f + 1], tiles[:, f + 1 : f + 2]) for f in range(WIN // LANE)],
        axis=1,
    )


def filter_strip(strips, row_ref, w_ref, wh_ref, g_ref, raw_ref, r_ref, pass_ref, arrive=()):
    for copy in arrive:
        copy.start()
    for i, ref in enumerate(strips * 2):
        raw_ref[XB * i : XB * (i + 1), :] = ref[...]
    own_bin = iota((BINS, 3 * XB), 0) == (iota((BINS, 3 * XB), 1) % XB) // ROWS
    for s in range(SCALES):
        for x in range(ROWS):
            for i in range(2):
                block = jnp.where(own_bin, row_ref[i, s, x : x + 1, :], 0.0).astype(BF16)
                at = XB * s + BINS * x
                r_ref[at : at + BINS, 3 * XB * i : 3 * XB * (i + 1)] = block
    pass_ref[...] = jnp.dot(r_ref[...], raw_ref[...], preferred_element_type=F32)
    mask = jnp.broadcast_to(strip_mask(strips[1]), (BINS, WIN))
    g_ref[SCALES * XB :, :] = mask.astype(BF16)
    mask = pltpu.roll(mask, WIN - EDGE, 1)[0:1] != 0
    for copy in arrive:
        copy.wait()
    for s in range(SCALES):
        rows = pass_ref[XB * s : XB * (s + 1), :]
        tiles = banded([rows[:, LANE * f : LANE * (f + 2)] for f in range(OWN // LANE)], w_ref[s])
        tiles += banded([jnp.concatenate([rows[:, :LANE], rows[:, OWN:]], axis=1)], wh_ref[s])
        filtered = jnp.concatenate(tiles, axis=1).astype(BF16).astype(F32)
        g = jnp.where(mask, filtered, 0.0).astype(BF16)
        g_ref[XB * s : XB * (s + 1), :] = g
        yield g


def beside_kernel(
    first_ref, second_ref, third_ref, row_ref, w_far, wh_far, g_far,
    raw_ref, r_ref, pass_ref, w_ref, wh_ref, g_ref, sem,
):
    strips = (first_ref, second_ref, third_ref)
    arrive = [
        pltpu.make_async_copy(w_far, w_ref, sem.at[0]),
        pltpu.make_async_copy(wh_far, wh_ref, sem.at[1]),
    ]
    for _ in filter_strip(strips, row_ref, w_ref, wh_ref, g_ref, raw_ref, r_ref, pass_ref, arrive):
        pass
    leave = pltpu.make_async_copy(g_ref, g_far, sem.at[2])
    leave.start()
    leave.wait()


def forward_kernel(
    up_ref, own_ref, down_ref, row_ref, w_ref, wh_ref, left_ref, right_ref,
    g_ref, out_ref, raw_ref, r_ref, pass_ref,
):
    slab = iota((BINS, ROWS * WIDE), 1) // WIDE
    parts = []
    strips = (up_ref, own_ref, down_ref)
    for g in filter_strip(strips, row_ref, w_ref, wh_ref, g_ref, raw_ref, r_ref, pass_ref):
        left = g[:, :OWN]
        right = jnp.concatenate(
            [
                (pltpu.roll(g, WIN - l, 1) if l else g)[:, :OWN].reshape(ROWS, BINS, OWN)
                for l in range(LAGS)
            ],
            axis=1,
        ).reshape(ROWS * WIDE, OWN)
        cross = lax.dot_general(left, right, (((1,), (1,)), ((), ())), preferred_element_type=F32)
        total = jnp.zeros((BINS, ROWS * WIDE), F32)
        for x in range(ROWS):
            total = jnp.where(slab == x, cross[BINS * x : BINS * (x + 1)], total)
        total = sum(total[:, LANE * i : LANE * (i + 1)] for i in range(ROWS * WIDE // LANE))
        parts.append(total[:, :WIDE] + total[:, WIDE:])
    table = jnp.concatenate(parts, axis=1)
    pieces = []
    for _ in range(3):
        piece = table.astype(BF16)
        table = table - piece.astype(F32)
        chosen = jnp.dot(left_ref[:, 0:BINS], piece, preferred_element_type=F32)
        pieces.append(chosen.astype(BF16) * right_ref[...])
    entries = lax.dot_general(
        jnp.concatenate(pieces, axis=0), spread_matrix(), (((1,), (1,)), ((), ())),
        preferred_element_type=F32,
    )
    entries = entries[0:PAIRS] + (entries[PAIRS : 2 * PAIRS] + entries[2 * PAIRS :])
    packed = jnp.concatenate(
        [entries[8 * a : 8 * (a + 1)] for a in range(GROUPS)]
        + [jnp.zeros((8, PACK - GROUPS * ENTRIES), F32)],
        axis=1,
    )
    out_ref[...] = jnp.broadcast_to(packed[None], out_ref.shape)


def backward_kernel(
    inverse_area,
    taps_ref, sums_ref, target_ref, weight_ref, left_ref, right_ref, own_ref, up_far, down_far, wa_far,
    corr_ref, out_ref, grad_ref, up_ref, down_ref, wa_ref, sem,
):
    copies = [
        pltpu.make_async_copy(up_far, up_ref, sem.at[0]),
        pltpu.make_async_copy(down_far, down_ref, sem.at[1]),
        pltpu.make_async_copy(wa_far, wa_ref, sem.at[2]),
    ]
    for copy in copies:
        copy.start()
    packed = sums_ref[0]
    for i in range(1, sums_ref.shape[0]):
        packed = packed + sums_ref[i]
    corr = inverse_area * jnp.concatenate(
        [packed[:, ENTRIES * a : ENTRIES * (a + 1)] for a in range(GROUPS)], axis=0
    )
    corr_ref[...] = corr
    grad = weight_ref[...] * (corr - target_ref[...])
    spread = spread_matrix()
    halves = []
    for piece in split2(grad):
        wide = jnp.dot(piece, spread, preferred_element_type=F32).astype(BF16)
        both = []
        for one, other in ((left_ref, right_ref), (right_ref, left_ref)):
            both.append(
                lax.dot_general(
                    one[:, 0:BINS], wide * other[...], (((0,), (0,)), ((), ())),
                    preferred_element_type=F32,
                )
            )
        halves.append(both)

    def mask_of(ref):
        return ref[SCALES * XB :, :].astype(F32) != 0

    masks = [mask_of(own_ref)]
    totals = [jnp.zeros((XB, LANE), F32)] * (OWN // LANE)
    for s in range(SCALES):
        at = slice(WIDE * s, WIDE * (s + 1))
        mix = jnp.concatenate(
            [jnp.concatenate([ahead[:, at], behind[:, at]], axis=1) for ahead, behind in halves],
            axis=0,
        )
        zero = jnp.zeros_like(mix)
        mix = jnp.concatenate(
            [jnp.concatenate([mix, zero], axis=1), jnp.concatenate([zero, mix], axis=1)], axis=0
        ).astype(BF16)
        for n, (k, ref) in enumerate(((1, own_ref), (0, up_ref), (2, down_ref))):
            if s == 0 and n:
                copies[n - 1].wait()
                masks.append(mask_of(ref))
            mask = masks[n]
            g = ref[XB * s : XB * (s + 1), :]
            ahead = [pltpu.roll(g, EDGE - l, 1) for l in range(LAGS)]
            behind = ahead[:1] + [pltpu.roll(g, EDGE + l, 1) for l in range(1, LAGS)]
            for x in range(0, ROWS, 2):
                maps = jnp.concatenate(
                    [v[BINS * y : BINS * (y + 1)] for y in (x, x + 1) for v in ahead + behind], axis=0
                )
                d = jnp.dot(mix, maps, preferred_element_type=F32)
                for i in range(2):
                    v = d[2 * BINS * i : 2 * BINS * (i + 1)]
                    grad_ref[s % 2, ROWS * k + x + i] = jnp.where(mask, v[:BINS] + v[BINS:], 0.0)
        rows = []
        for x in range(ROWS):
            acc = taps_ref[s, TAPS - 1] * grad_ref[s % 2, x]
            for a in range(1, TAPS):
                acc = acc + taps_ref[s, TAPS - 1 - a] * grad_ref[s % 2, x + a]
            rows.append(acc)
        rows = jnp.concatenate(rows, axis=0)
        if s == 0:
            copies[2].wait()
        tiles = banded([rows[:, LANE * c : LANE * (c + 2)] for c in range(OWN // LANE)], wa_ref[s])
        totals = [total + tile for total, tile in zip(totals, tiles)]
    for c, total in enumerate(totals):
        for x in range(ROWS):
            at = pl.ds(ROWS * c + x, BINS, stride=ROWS * OWN // LANE)
            out_ref[at, :] = total[BINS * x : BINS * (x + 1)]


def struct(shape, dtype):
    return jax.ShapeDtypeStruct(shape, dtype)


VMEM = pl.BlockSpec(memory_space=pltpu.VMEM)
HBM = pl.BlockSpec(memory_space=pltpu.HBM)
COLUMN = (SCALES, 2 * LANE, 2 * LANE)
MAPS = (SCALES * XB + BINS, WIN)


def far(v):
    return pltpu.with_memory_space_constraint(v, pltpu.HBM)


def limit(mib):
    return pltpu.CompilerParams(vmem_limit_bytes=mib * 1024 * 1024)


def cost(flops, moved):
    return pl.CostEstimate(flops=flops, bytes_accessed=moved, transcendentals=0)


def matrices(filter_taps, bin_pairs):
    pairs = jnp.pad(bin_pairs, ((0, PAIRS - bin_pairs.shape[0]), (0, 0)), constant_values=-1)
    column = struct(COLUMN, BF16)
    return pl.pallas_call(
        matrices_kernel,
        in_specs=[SMEM, VMEM],
        out_shape=(
            struct((2, SCALES, ROWS, 3 * XB), F32),
            column,
            column,
            struct((PAIRS, TABLE), BF16),
            struct((PAIRS, TABLE), BF16),
            pltpu.HBM(COLUMN, BF16),
            pltpu.HBM(COLUMN, BF16),
            pltpu.HBM(COLUMN, BF16),
        ),
        out_specs=[VMEM] * 5 + [HBM] * 3,
        scratch_shapes=[pltpu.VMEM(COLUMN, BF16), pltpu.SemaphoreType.DMA((3,))],
        compiler_params=limit(32),
        cost_estimate=cost(20_000_000, 4_000_000),
        name="matrices",
    )(filter_taps, pairs)


def scratch():
    return [
        pltpu.VMEM((6 * XB, WIN), BF16),
        pltpu.VMEM((SCALES * XB, 6 * XB), BF16),
        pltpu.VMEM((SCALES * XB, WIN), F32),
    ]


def forward(strips, row, w, wh, left, right, copies):
    return pl.pallas_call(
        forward_kernel,
        out_shape=(struct(MAPS, BF16), struct((copies, 8, PACK), F32)),
        scratch_shapes=scratch(),
        compiler_params=limit(32),
        name="forward",
    )(*strips, row, w, wh, left, right)


def beside(strips, row, w, wh):
    return pl.pallas_call(
        beside_kernel,
        in_specs=[VMEM] * 4 + [HBM] * 2,
        out_specs=HBM,
        out_shape=pltpu.HBM(MAPS, BF16),
        scratch_shapes=scratch()
        + [
            pltpu.VMEM(COLUMN, BF16),
            pltpu.VMEM(COLUMN, BF16),
            pltpu.VMEM(MAPS, BF16),
            pltpu.SemaphoreType.DMA((3,)),
        ],
        compiler_params=limit(32),
        cost_estimate=cost(2_000_000_000, 8_000_000),
        name="beside",
    )(*strips, row, far(w), far(wh))


def backward(inverse_area, taps, sums, target, weight, left, right, wa, above, own, below):
    return pl.pallas_call(
        lambda *refs: backward_kernel(inverse_area, *refs),
        in_specs=[SMEM] + [VMEM] * 6 + [HBM] * 3,
        out_shape=(struct((PAIRS, ENTRIES), F32), struct((XB * OWN // LANE, LANE), F32)),
        scratch_shapes=[
            pltpu.VMEM((2, 3 * ROWS, BINS, WIN), F32),
            pltpu.VMEM(MAPS, BF16),
            pltpu.VMEM(MAPS, BF16),
            pltpu.VMEM(COLUMN, BF16),
            pltpu.SemaphoreType.DMA((3,)),
        ],
        compiler_params=limit(32),
        name="backward",
    )(taps, sums, target, weight, left, right, own, far(above), far(below), far(wa))


def per_device(lensing_maps, filter_taps, survey_mask, bin_pairs, target_corr, pair_weight):
    strip = lensing_maps[0]
    rows, cols = strip.shape
    bins = lax.axis_size("bin")
    sky = lax.axis_size("sky")
    pairs = bin_pairs.shape[0]
    inverse_area = 1.0 / (rows * sky * cols)
    down_perm = [(i, i + 1) for i in range(sky - 1)]
    up_perm = [(i + 1, i) for i in range(sky - 1)]

    def padded(v):
        return jnp.pad(v.reshape(pairs, ENTRIES), ((0, PAIRS - pairs), (0, 0)))

    windows = pl.pallas_call(
        windows_kernel,
        out_shape=struct((XB, WIN), BF16),
        compiler_params=limit(60),
        name="windows",
    )(strip, survey_mask)
    own = lax.all_to_all(windows, "bin", 0, 0, tiled=True)
    made = matrices(filter_taps, bin_pairs)
    own, (row, w, wh, left, right, w_far, wh_far, wa) = lax.optimization_barrier((own, made))
    above = lax.ppermute(own, "sky", down_perm)
    below = lax.ppermute(own, "sky", up_perm)
    above2 = lax.ppermute(own, "sky", [(i, i + 2) for i in range(sky - 2)])
    below2 = lax.ppermute(own, "sky", [(i + 2, i) for i in range(sky - 2)])
    g, partial = forward((above, own, below), row, w, wh, left, right, sky)
    g_above = beside((above2, above, own), row, w_far, wh_far)
    g_below = beside((own, below, below2), row, w_far, wh_far)
    partial = lax.all_to_all(partial, "sky", 0, 0, tiled=True)
    partial = jnp.broadcast_to(jnp.sum(partial, axis=0)[None], (bins,) + partial.shape[1:])
    partial = lax.all_to_all(partial, "bin", 0, 0, tiled=True)
    corr, tile_grad = backward(
        inverse_area, filter_taps, partial, padded(target_corr), padded(pair_weight),
        left, right, wa, g_above, g, g_below,
    )
    back = lax.all_to_all(tile_grad, "bin", 0, 0, tiled=True)
    map_grad = jnp.transpose(back.reshape(cols // LANE, rows, LANE), (1, 0, 2)).reshape(1, rows, cols)
    return (corr[:pairs].reshape(target_corr.shape), map_grad)


def solution(mesh):
    placed = (P("bin", "sky", None), P(), P("sky", None), P(), P(), P())
    return jax.shard_map(
        per_device,
        mesh=mesh,
        in_specs=placed,
        out_specs=(P(), P("bin", "sky", None)),
        check_vma=False,
    )
```

```python
import jax
import jax.numpy as jnp
from jax import lax
from jax.experimental import pallas as pl
from jax.experimental.pallas import tpu as pltpu
from jax.sharding import PartitionSpec as P

F32 = jnp.float32
BF16 = jnp.bfloat16
HIGH = lax.Precision.HIGHEST

BINS = 16
SCALES = 5
TAPS = 17
LAGS = 4
ROWS = 8
OWN = 512
LANE = 128
EDGE = 64
WIN = OWN + 2 * EDGE
XB = ROWS * BINS
WIDE = LAGS * BINS
TABLE = SCALES * WIDE
ENTRIES = SCALES * LAGS
PAIRS = 144
GROUPS = PAIRS // 8
PACK = 384


def full(shape):
    return pl.BlockSpec(shape, lambda *_: (0,) * len(shape))


def per_scale(shape):
    return pl.BlockSpec((1,) + shape, lambda s: (s,) + (0,) * len(shape))


SMEM = pl.BlockSpec(memory_space=pltpu.SMEM)


def split2(v):
    hi = v.astype(BF16)
    return hi, (v - hi.astype(F32)).astype(BF16)


def iota(shape, dim):
    return lax.broadcasted_iota(jnp.int32, shape, dim)


def windows_kernel(x_ref, mask_ref, out_ref):
    tiles = mask_ref.shape[1]
    tiles = jnp.concatenate([mask_ref[...].astype(F32), jnp.zeros((1, LANE - tiles), F32)], axis=1)
    tiles = jnp.broadcast_to(tiles, (ROWS, LANE))
    corner = (iota((ROWS, LANE), 0) == 0) & (iota((ROWS, LANE), 1) <= WIN // LANE)
    x = pltpu.roll(x_ref[...].astype(F32), EDGE, 1)
    count = x.shape[1] // OWN
    left = iota((ROWS, LANE), 1) < EDGE
    head = jnp.where(left, 0.0, x[:, :LANE])
    tail = jnp.where(left, x[:, :LANE], 0.0)

    def window(b):
        first = head if b == 0 else x[:, b * OWN : b * OWN + LANE]
        first = jnp.where(corner, pltpu.roll(tiles, (1 - b * (OWN // LANE)) % LANE, 1), first)
        if b == count - 1:
            return jnp.concatenate([first, x[:, b * OWN + LANE :], tail], axis=1)
        return jnp.concatenate([first, x[:, b * OWN + LANE : b * OWN + WIN]], axis=1)

    for p in range(count // 2):
        pair = jnp.concatenate([window(2 * p), window(2 * p + 1)], axis=0)
        out_ref[2 * ROWS * p : 2 * ROWS * (p + 1), :] = pair.astype(BF16)


def matrices_kernel(
    taps_ref, pairs_ref, row_ref, w_ref, wh_ref, left_ref, right_ref,
    w_far, wh_far, wa_far, wa_ref, sem,
):
    for c, out_ref in enumerate((left_ref, right_ref)):
        bins = iota(out_ref.shape, 1) % BINS
        out_ref[...] = (pairs_ref[:, c : c + 1] == bins).astype(F32).astype(BF16)

    lane = iota((8, LANE), 1)
    n = iota((2 * LANE, LANE), 0)
    o = iota((2 * LANE, LANE), 1)
    k = o + 72 - n
    middle = (k >= 0) & (k < TAPS)
    k = jnp.where((o < EDGE) == (n >= LANE), jnp.where(o < EDGE, o + 200, o - 56) - n, -1)
    ends = (k >= 0) & (k < TAPS)

    def toeplitz(base, shift, valid):
        wide = jnp.broadcast_to(base[0:1], (2 * LANE, LANE))
        return jnp.where(valid, pltpu.roll(wide, shift, 1, stride=1, stride_axis=0), 0.0).astype(BF16)

    q = iota((ROWS, 3 * XB), 0)
    m = iota((ROWS, 3 * XB), 1)
    row_tap = m % ROWS - q + ROWS * (m // XB)
    def one(s, carry):
        base = jnp.zeros((8, LANE), F32)
        flipped = jnp.zeros((8, LANE), F32)
        rows = jnp.zeros(row_tap.shape, F32)
        for a in range(TAPS):
            tap = taps_ref[s, a]
            base = jnp.where(lane == a, tap, base)
            flipped = jnp.where(lane == TAPS - 1 - a, tap, flipped)
            rows = jnp.where(row_tap == a, tap, rows)
        for i in range(2):
            if i:
                base, flipped, rows = (
                    v - v.astype(BF16).astype(F32) for v in (base, flipped, rows)
                )
            base_i, flipped_i, rows_i = (v.astype(BF16).astype(F32) for v in (base, flipped, rows))
            at = slice(LANE * i, LANE * (i + 1))
            w_ref[s, :, at] = toeplitz(flipped_i, LANE - 72, middle)
            wh_ref[s, :, at] = toeplitz(flipped_i, 56, ends)
            wa_ref[s, :, at] = toeplitz(base_i, LANE - 72, middle)
            row_ref[i, s] = rows_i
        return carry

    lax.fori_loop(0, SCALES, one, 0)
    copies = [
        pltpu.make_async_copy(near, far, sem.at[i])
        for i, (near, far) in enumerate(((w_ref, w_far), (wh_ref, wh_far), (wa_ref, wa_far)))
    ]
    for copy in copies:
        copy.start()
    for copy in copies:
        copy.wait()


def banded(slabs, w):
    count = len(slabs)
    halves = [split2(slab) for slab in slabs]
    stacked = jnp.concatenate([h[i] for i in range(2) for h in halves], axis=0)
    d = jnp.dot(stacked, w, preferred_element_type=F32)
    d = d[:, :LANE] + d[:, LANE:]
    return [d[XB * f : XB * (f + 1)] + d[XB * (count + f) : XB * (count + f + 1)] for f in range(count)]


def spread_matrix():
    return (iota((ENTRIES, TABLE), 1) // BINS == iota((ENTRIES, TABLE), 0)).astype(F32).astype(BF16)


def strip_mask(raw_ref):
    tiles = raw_ref[0:BINS, 0:LANE].astype(F32)[0:1]
    left = iota((1, LANE), 1) < EDGE
    return jnp.concatenate(
        [jnp.where(left, tiles[:, f : f + 1], tiles[:, f + 1 : f + 2]) for f in range(WIN // LANE)],
        axis=1,
    )


def filter_strip(strips, row_ref, w_ref, wh_ref, g_ref, raw_ref, r_ref, pass_ref, arrive=()):
    for copy in arrive:
        copy.start()
    for i, ref in enumerate(strips * 2):
        raw_ref[XB * i : XB * (i + 1), :] = ref[...]
    own_bin = iota((BINS, 3 * XB), 0) == (iota((BINS, 3 * XB), 1) % XB) // ROWS
    for s in range(SCALES):
        for x in range(ROWS):
            for i in range(2):
                block = jnp.where(own_bin, row_ref[i, s, x : x + 1, :], 0.0).astype(BF16)
                at = XB * s + BINS * x
                r_ref[at : at + BINS, 3 * XB * i : 3 * XB * (i + 1)] = block
    pass_ref[...] = jnp.dot(r_ref[...], raw_ref[...], preferred_element_type=F32)
    mask = jnp.broadcast_to(strip_mask(strips[1]), (BINS, WIN))
    g_ref[SCALES * XB :, :] = mask.astype(BF16)
    mask = pltpu.roll(mask, WIN - EDGE, 1)[0:1] != 0
    for copy in arrive:
        copy.wait()
    for s in range(SCALES):
        rows = pass_ref[XB * s : XB * (s + 1), :]
        tiles = banded([rows[:, LANE * f : LANE * (f + 2)] for f in range(OWN // LANE)], w_ref[s])
        tiles += banded([jnp.concatenate([rows[:, :LANE], rows[:, OWN:]], axis=1)], wh_ref[s])
        filtered = jnp.concatenate(tiles, axis=1).astype(BF16).astype(F32)
        g = jnp.where(mask, filtered, 0.0).astype(BF16)
        g_ref[XB * s : XB * (s + 1), :] = g
        yield g


def beside_kernel(
    first_ref, second_ref, third_ref, row_ref, w_far, wh_far, g_far,
    raw_ref, r_ref, pass_ref, w_ref, wh_ref, g_ref, sem,
):
    strips = (first_ref, second_ref, third_ref)
    arrive = [
        pltpu.make_async_copy(w_far, w_ref, sem.at[0]),
        pltpu.make_async_copy(wh_far, wh_ref, sem.at[1]),
    ]
    for _ in filter_strip(strips, row_ref, w_ref, wh_ref, g_ref, raw_ref, r_ref, pass_ref, arrive):
        pass
    leave = pltpu.make_async_copy(g_ref, g_far, sem.at[2])
    leave.start()
    leave.wait()


def forward_kernel(
    up_ref, own_ref, down_ref, row_ref, w_ref, wh_ref, left_ref, right_ref,
    g_ref, out_ref, raw_ref, r_ref, pass_ref,
):
    slab = iota((BINS, ROWS * WIDE), 1) // WIDE
    parts = []
    strips = (up_ref, own_ref, down_ref)
    for g in filter_strip(strips, row_ref, w_ref, wh_ref, g_ref, raw_ref, r_ref, pass_ref):
        left = g[:, :OWN]
        right = jnp.concatenate(
            [
                (pltpu.roll(g, WIN - l, 1) if l else g)[:, :OWN].reshape(ROWS, BINS, OWN)
                for l in range(LAGS)
            ],
            axis=1,
        ).reshape(ROWS * WIDE, OWN)
        cross = lax.dot_general(left, right, (((1,), (1,)), ((), ())), preferred_element_type=F32)
        total = jnp.zeros((BINS, ROWS * WIDE), F32)
        for x in range(ROWS):
            total = jnp.where(slab == x, cross[BINS * x : BINS * (x + 1)], total)
        total = sum(total[:, LANE * i : LANE * (i + 1)] for i in range(ROWS * WIDE // LANE))
        parts.append(total[:, :WIDE] + total[:, WIDE:])
    table = jnp.concatenate(parts, axis=1)
    pieces = []
    for _ in range(3):
        piece = table.astype(BF16)
        table = table - piece.astype(F32)
        chosen = jnp.dot(left_ref[:, 0:BINS], piece, preferred_element_type=F32)
        pieces.append(chosen.astype(BF16) * right_ref[...])
    entries = lax.dot_general(
        jnp.concatenate(pieces, axis=0), spread_matrix(), (((1,), (1,)), ((), ())),
        preferred_element_type=F32,
    )
    entries = entries[0:PAIRS] + (entries[PAIRS : 2 * PAIRS] + entries[2 * PAIRS :])
    packed = jnp.concatenate(
        [entries[8 * a : 8 * (a + 1)] for a in range(GROUPS)]
        + [jnp.zeros((8, PACK - GROUPS * ENTRIES), F32)],
        axis=1,
    )
    out_ref[...] = jnp.broadcast_to(packed[None], out_ref.shape)


def backward_kernel(
    inverse_area,
    taps_ref, sums_ref, target_ref, weight_ref, left_ref, right_ref, own_ref, up_far, down_far, wa_far,
    corr_ref, out_ref, grad_ref, up_ref, down_ref, wa_ref, sem,
):
    copies = [
        pltpu.make_async_copy(up_far, up_ref, sem.at[0]),
        pltpu.make_async_copy(down_far, down_ref, sem.at[1]),
        pltpu.make_async_copy(wa_far, wa_ref, sem.at[2]),
    ]
    for copy in copies:
        copy.start()
    packed = sums_ref[0]
    for i in range(1, sums_ref.shape[0]):
        packed = packed + sums_ref[i]
    corr = inverse_area * jnp.concatenate(
        [packed[:, ENTRIES * a : ENTRIES * (a + 1)] for a in range(GROUPS)], axis=0
    )
    corr_ref[...] = corr
    grad = weight_ref[...] * (corr - target_ref[...])
    spread = spread_matrix()
    halves = []
    for piece in split2(grad):
        wide = jnp.dot(piece, spread, preferred_element_type=F32).astype(BF16)
        both = []
        for one, other in ((left_ref, right_ref), (right_ref, left_ref)):
            both.append(
                lax.dot_general(
                    one[:, 0:BINS], wide * other[...], (((0,), (0,)), ((), ())),
                    preferred_element_type=F32,
                )
            )
        halves.append(both)

    def mask_of(ref):
        return ref[SCALES * XB :, :].astype(F32) != 0

    masks = [mask_of(own_ref)]
    totals = [jnp.zeros((XB, LANE), F32)] * (OWN // LANE)
    for s in range(SCALES):
        at = slice(WIDE * s, WIDE * (s + 1))
        mix = jnp.concatenate(
            [jnp.concatenate([ahead[:, at], behind[:, at]], axis=1) for ahead, behind in halves],
            axis=0,
        )
        zero = jnp.zeros_like(mix)
        mix = jnp.concatenate(
            [jnp.concatenate([mix, zero], axis=1), jnp.concatenate([zero, mix], axis=1)], axis=0
        ).astype(BF16)
        for n, (k, ref) in enumerate(((1, own_ref), (0, up_ref), (2, down_ref))):
            if s == 0 and n:
                copies[n - 1].wait()
                masks.append(mask_of(ref))
            mask = masks[n]
            g = ref[XB * s : XB * (s + 1), :]
            ahead = [pltpu.roll(g, EDGE - l, 1) for l in range(LAGS)]
            behind = ahead[:1] + [pltpu.roll(g, EDGE + l, 1) for l in range(1, LAGS)]
            for x in range(0, ROWS, 2):
                maps = jnp.concatenate(
                    [v[BINS * y : BINS * (y + 1)] for y in (x, x + 1) for v in ahead + behind], axis=0
                )
                d = jnp.dot(mix, maps, preferred_element_type=F32)
                for i in range(2):
                    v = d[2 * BINS * i : 2 * BINS * (i + 1)]
                    grad_ref[s % 2, ROWS * k + x + i] = jnp.where(mask, v[:BINS] + v[BINS:], 0.0)
        rows = []
        for x in range(ROWS):
            acc = taps_ref[s, TAPS - 1] * grad_ref[s % 2, x]
            for a in range(1, TAPS):
                acc = acc + taps_ref[s, TAPS - 1 - a] * grad_ref[s % 2, x + a]
            rows.append(acc)
        rows = jnp.concatenate(rows, axis=0)
        if s == 0:
            copies[2].wait()
        tiles = banded([rows[:, LANE * c : LANE * (c + 2)] for c in range(OWN // LANE)], wa_ref[s])
        totals = [total + tile for total, tile in zip(totals, tiles)]
    for c, total in enumerate(totals):
        for x in range(ROWS):
            at = pl.ds(ROWS * c + x, BINS, stride=ROWS * OWN // LANE)
            out_ref[at, :] = total[BINS * x : BINS * (x + 1)]


def struct(shape, dtype):
    return jax.ShapeDtypeStruct(shape, dtype)


VMEM = pl.BlockSpec(memory_space=pltpu.VMEM)
HBM = pl.BlockSpec(memory_space=pltpu.HBM)
COLUMN = (SCALES, 2 * LANE, 2 * LANE)
MAPS = (SCALES * XB + BINS, WIN)


def far(v):
    return pltpu.with_memory_space_constraint(v, pltpu.HBM)


def limit(mib):
    return pltpu.CompilerParams(vmem_limit_bytes=mib * 1024 * 1024)


def cost(flops, moved):
    return pl.CostEstimate(flops=flops, bytes_accessed=moved, transcendentals=0)


def matrices(filter_taps, bin_pairs):
    pairs = jnp.pad(bin_pairs, ((0, PAIRS - bin_pairs.shape[0]), (0, 0)), constant_values=-1)
    column = struct(COLUMN, BF16)
    return pl.pallas_call(
        matrices_kernel,
        in_specs=[SMEM, VMEM],
        out_shape=(
            struct((2, SCALES, ROWS, 3 * XB), F32),
            column,
            column,
            struct((PAIRS, TABLE), BF16),
            struct((PAIRS, TABLE), BF16),
            pltpu.HBM(COLUMN, BF16),
            pltpu.HBM(COLUMN, BF16),
            pltpu.HBM(COLUMN, BF16),
        ),
        out_specs=[VMEM] * 5 + [HBM] * 3,
        scratch_shapes=[pltpu.VMEM(COLUMN, BF16), pltpu.SemaphoreType.DMA((3,))],
        compiler_params=limit(32),
        cost_estimate=cost(20_000_000, 4_000_000),
        name="matrices",
    )(filter_taps, pairs)


def scratch():
    return [
        pltpu.VMEM((6 * XB, WIN), BF16),
        pltpu.VMEM((SCALES * XB, 6 * XB), BF16),
        pltpu.VMEM((SCALES * XB, WIN), F32),
    ]


def forward(strips, row, w, wh, left, right, copies):
    return pl.pallas_call(
        forward_kernel,
        out_shape=(struct(MAPS, BF16), struct((copies, 8, PACK), F32)),
        scratch_shapes=scratch(),
        compiler_params=limit(32),
        name="forward",
    )(*strips, row, w, wh, left, right)


def beside(strips, row, w, wh):
    return pl.pallas_call(
        beside_kernel,
        in_specs=[VMEM] * 4 + [HBM] * 2,
        out_specs=HBM,
        out_shape=pltpu.HBM(MAPS, BF16),
        scratch_shapes=scratch()
        + [
            pltpu.VMEM(COLUMN, BF16),
            pltpu.VMEM(COLUMN, BF16),
            pltpu.VMEM(MAPS, BF16),
            pltpu.SemaphoreType.DMA((3,)),
        ],
        compiler_params=limit(32),
        cost_estimate=cost(2_000_000_000, 8_000_000),
        name="beside",
    )(*strips, row, far(w), far(wh))


def backward(inverse_area, taps, sums, target, weight, left, right, wa, above, own, below):
    return pl.pallas_call(
        lambda *refs: backward_kernel(inverse_area, *refs),
        in_specs=[SMEM] + [VMEM] * 6 + [HBM] * 3,
        out_shape=(struct((PAIRS, ENTRIES), F32), struct((XB * OWN // LANE, LANE), F32)),
        scratch_shapes=[
            pltpu.VMEM((2, 3 * ROWS, BINS, WIN), F32),
            pltpu.VMEM(MAPS, BF16),
            pltpu.VMEM(MAPS, BF16),
            pltpu.VMEM(COLUMN, BF16),
            pltpu.SemaphoreType.DMA((3,)),
        ],
        compiler_params=limit(32),
        name="backward",
    )(taps, sums, target, weight, left, right, own, far(above), far(below), far(wa))


def per_device(lensing_maps, filter_taps, survey_mask, bin_pairs, target_corr, pair_weight):
    strip = lensing_maps[0]
    rows, cols = strip.shape
    bins = lax.axis_size("bin")
    sky = lax.axis_size("sky")
    pairs = bin_pairs.shape[0]
    inverse_area = 1.0 / (rows * sky * cols)
    down_perm = [(i, i + 1) for i in range(sky - 1)]
    up_perm = [(i + 1, i) for i in range(sky - 1)]

    def padded(v):
        return jnp.pad(v.reshape(pairs, ENTRIES), ((0, PAIRS - pairs), (0, 0)))

    windows = pl.pallas_call(
        windows_kernel,
        out_shape=struct((XB, WIN), BF16),
        compiler_params=limit(60),
        name="windows",
    )(strip, survey_mask)
    own = lax.all_to_all(windows, "bin", 0, 0, tiled=True)
    made = matrices(filter_taps, bin_pairs)
    own, (row, w, wh, left, right, w_far, wh_far, wa) = lax.optimization_barrier((own, made))
    above = lax.ppermute(own, "sky", down_perm)
    below = lax.ppermute(own, "sky", up_perm)
    above2 = lax.ppermute(own, "sky", [(i, i + 2) for i in range(sky - 2)])
    below2 = lax.ppermute(own, "sky", [(i + 2, i) for i in range(sky - 2)])
    g, partial = forward((above, own, below), row, w, wh, left, right, bins)
    g_above = beside((above2, above, own), row, w_far, wh_far)
    g_below = beside((own, below, below2), row, w_far, wh_far)
    partial = lax.all_to_all(partial, "bin", 0, 0, tiled=True)
    partial = jnp.broadcast_to(jnp.sum(partial, axis=0)[None], (sky,) + partial.shape[1:])
    partial = lax.all_to_all(partial, "sky", 0, 0, tiled=True)
    corr, tile_grad = backward(
        inverse_area, filter_taps, partial, padded(target_corr), padded(pair_weight),
        left, right, wa, g_above, g, g_below,
    )
    back = lax.all_to_all(tile_grad, "bin", 0, 0, tiled=True)
    map_grad = jnp.transpose(back.reshape(cols // LANE, rows, LANE), (1, 0, 2)).reshape(1, rows, cols)
    return (corr[:pairs].reshape(target_corr.shape), map_grad)


def solution(mesh):
    placed = (P("bin", "sky", None), P(), P("sky", None), P(), P(), P())
    return jax.shard_map(
        per_device,
        mesh=mesh,
        in_specs=placed,
        out_specs=(P(), P("bin", "sky", None)),
        check_vma=False,
    )
```

```python
import jax
import jax.numpy as jnp
from jax import lax
from jax.experimental import pallas as pl
from jax.experimental.pallas import tpu as pltpu
from jax.sharding import PartitionSpec as P

F32 = jnp.float32
BF16 = jnp.bfloat16
HIGH = lax.Precision.HIGHEST

BINS = 16
SCALES = 5
TAPS = 17
LAGS = 4
ROWS = 8
OWN = 512
LANE = 128
EDGE = 64
WIN = OWN + 2 * EDGE
XB = ROWS * BINS
WIDE = LAGS * BINS
TABLE = SCALES * WIDE
ENTRIES = SCALES * LAGS
PAIRS = 144
GROUPS = PAIRS // 8
PACK = 384


def full(shape):
    return pl.BlockSpec(shape, lambda *_: (0,) * len(shape))


def per_scale(shape):
    return pl.BlockSpec((1,) + shape, lambda s: (s,) + (0,) * len(shape))


SMEM = pl.BlockSpec(memory_space=pltpu.SMEM)


def split2(v):
    hi = v.astype(BF16)
    return hi, (v - hi.astype(F32)).astype(BF16)


def iota(shape, dim):
    return lax.broadcasted_iota(jnp.int32, shape, dim)


def windows_kernel(x_ref, mask_ref, out_ref):
    tiles = mask_ref.shape[1]
    tiles = jnp.concatenate([mask_ref[...].astype(F32), jnp.zeros((1, LANE - tiles), F32)], axis=1)
    tiles = jnp.broadcast_to(tiles, (ROWS, LANE))
    corner = (iota((ROWS, LANE), 0) == 0) & (iota((ROWS, LANE), 1) <= WIN // LANE)
    x = pltpu.roll(x_ref[...].astype(F32), EDGE, 1)
    count = x.shape[1] // OWN
    left = iota((ROWS, LANE), 1) < EDGE
    head = jnp.where(left, 0.0, x[:, :LANE])
    tail = jnp.where(left, x[:, :LANE], 0.0)

    def window(b):
        first = head if b == 0 else x[:, b * OWN : b * OWN + LANE]
        first = jnp.where(corner, pltpu.roll(tiles, (1 - b * (OWN // LANE)) % LANE, 1), first)
        if b == count - 1:
            return jnp.concatenate([first, x[:, b * OWN + LANE :], tail], axis=1)
        return jnp.concatenate([first, x[:, b * OWN + LANE : b * OWN + WIN]], axis=1)

    for p in range(count // 2):
        pair = jnp.concatenate([window(2 * p), window(2 * p + 1)], axis=0)
        out_ref[2 * ROWS * p : 2 * ROWS * (p + 1), :] = pair.astype(BF16)


def matrices_kernel(
    taps_ref, pairs_ref, row_ref, w_ref, wh_ref, left_ref, right_ref,
    w_far, wh_far, wa_far, wa_ref, sem,
):
    for c, out_ref in enumerate((left_ref, right_ref)):
        bins = iota(out_ref.shape, 1) % BINS
        out_ref[...] = (pairs_ref[:, c : c + 1] == bins).astype(F32).astype(BF16)

    lane = iota((8, LANE), 1)
    n = iota((2 * LANE, LANE), 0)
    o = iota((2 * LANE, LANE), 1)
    k = o + 72 - n
    middle = (k >= 0) & (k < TAPS)
    k = jnp.where((o < EDGE) == (n >= LANE), jnp.where(o < EDGE, o + 200, o - 56) - n, -1)
    ends = (k >= 0) & (k < TAPS)

    def toeplitz(base, shift, valid):
        wide = jnp.broadcast_to(base[0:1], (2 * LANE, LANE))
        return jnp.where(valid, pltpu.roll(wide, shift, 1, stride=1, stride_axis=0), 0.0).astype(BF16)

    q = iota((ROWS, 3 * XB), 0)
    m = iota((ROWS, 3 * XB), 1)
    row_tap = m % ROWS - q + ROWS * (m // XB)
    def one(s, carry):
        base = jnp.zeros((8, LANE), F32)
        flipped = jnp.zeros((8, LANE), F32)
        rows = jnp.zeros(row_tap.shape, F32)
        for a in range(TAPS):
            tap = taps_ref[s, a]
            base = jnp.where(lane == a, tap, base)
            flipped = jnp.where(lane == TAPS - 1 - a, tap, flipped)
            rows = jnp.where(row_tap == a, tap, rows)
        for i in range(2):
            if i:
                base, flipped, rows = (
                    v - v.astype(BF16).astype(F32) for v in (base, flipped, rows)
                )
            base_i, flipped_i, rows_i = (v.astype(BF16).astype(F32) for v in (base, flipped, rows))
            at = slice(LANE * i, LANE * (i + 1))
            w_ref[s, :, at] = toeplitz(flipped_i, LANE - 72, middle)
            wh_ref[s, :, at] = toeplitz(flipped_i, 56, ends)
            wa_ref[s, :, at] = toeplitz(base_i, LANE - 72, middle)
            row_ref[i, s] = rows_i
        return carry

    lax.fori_loop(0, SCALES, one, 0)
    copies = [
        pltpu.make_async_copy(near, far, sem.at[i])
        for i, (near, far) in enumerate(((w_ref, w_far), (wh_ref, wh_far), (wa_ref, wa_far)))
    ]
    for copy in copies:
        copy.start()
    for copy in copies:
        copy.wait()


def banded(slabs, w):
    count = len(slabs)
    halves = [split2(slab) for slab in slabs]
    stacked = jnp.concatenate([h[i] for i in range(2) for h in halves], axis=0)
    d = jnp.dot(stacked, w, preferred_element_type=F32)
    d = d[:, :LANE] + d[:, LANE:]
    return [d[XB * f : XB * (f + 1)] + d[XB * (count + f) : XB * (count + f + 1)] for f in range(count)]


def spread_matrix():
    return (iota((ENTRIES, TABLE), 1) // BINS == iota((ENTRIES, TABLE), 0)).astype(F32).astype(BF16)


def strip_mask(raw_ref):
    tiles = raw_ref[0:BINS, 0:LANE].astype(F32)[0:1]
    left = iota((1, LANE), 1) < EDGE
    return jnp.concatenate(
        [jnp.where(left, tiles[:, f : f + 1], tiles[:, f + 1 : f + 2]) for f in range(WIN // LANE)],
        axis=1,
    )


def filter_strip(strips, row_ref, w_ref, wh_ref, g_ref, raw_ref, r_ref, pass_ref, arrive=()):
    for copy in arrive:
        copy.start()
    for i, ref in enumerate(strips * 2):
        raw_ref[XB * i : XB * (i + 1), :] = ref[...]
    own_bin = iota((BINS, 3 * XB), 0) == (iota((BINS, 3 * XB), 1) % XB) // ROWS
    for s in range(SCALES):
        for x in range(ROWS):
            for i in range(2):
                block = jnp.where(own_bin, row_ref[i, s, x : x + 1, :], 0.0).astype(BF16)
                at = XB * s + BINS * x
                r_ref[at : at + BINS, 3 * XB * i : 3 * XB * (i + 1)] = block
    pass_ref[...] = jnp.dot(r_ref[...], raw_ref[...], preferred_element_type=F32)
    mask = jnp.broadcast_to(strip_mask(strips[1]), (BINS, WIN))
    g_ref[SCALES * XB :, :] = mask.astype(BF16)
    mask = pltpu.roll(mask, WIN - EDGE, 1)[0:1] != 0
    for copy in arrive:
        copy.wait()
    for s in range(SCALES):
        rows = pass_ref[XB * s : XB * (s + 1), :]
        tiles = banded([rows[:, LANE * f : LANE * (f + 2)] for f in range(OWN // LANE)], w_ref[s])
        tiles += banded([jnp.concatenate([rows[:, :LANE], rows[:, OWN:]], axis=1)], wh_ref[s])
        filtered = jnp.concatenate(tiles, axis=1).astype(BF16).astype(F32)
        g = jnp.where(mask, filtered, 0.0).astype(BF16)
        g_ref[XB * s : XB * (s + 1), :] = g
        yield g


def beside_kernel(
    first_ref, second_ref, third_ref, row_ref, w_far, wh_far, g_far,
    raw_ref, r_ref, pass_ref, w_ref, wh_ref, g_ref, sem,
):
    strips = (first_ref, second_ref, third_ref)
    arrive = [
        pltpu.make_async_copy(w_far, w_ref, sem.at[0]),
        pltpu.make_async_copy(wh_far, wh_ref, sem.at[1]),
    ]
    for _ in filter_strip(strips, row_ref, w_ref, wh_ref, g_ref, raw_ref, r_ref, pass_ref, arrive):
        pass
    leave = pltpu.make_async_copy(g_ref, g_far, sem.at[2])
    leave.start()
    leave.wait()


def forward_kernel(
    up_ref, own_ref, down_ref, row_ref, w_ref, wh_ref, left_ref, right_ref,
    g_ref, out_ref, raw_ref, r_ref, pass_ref,
):
    slab = iota((BINS, ROWS * WIDE), 1) // WIDE
    parts = []
    strips = (up_ref, own_ref, down_ref)
    for g in filter_strip(strips, row_ref, w_ref, wh_ref, g_ref, raw_ref, r_ref, pass_ref):
        left = g[:, :OWN]
        right = jnp.concatenate(
            [
                (pltpu.roll(g, WIN - l, 1) if l else g)[:, :OWN].reshape(ROWS, BINS, OWN)
                for l in range(LAGS)
            ],
            axis=1,
        ).reshape(ROWS * WIDE, OWN)
        cross = lax.dot_general(left, right, (((1,), (1,)), ((), ())), preferred_element_type=F32)
        total = jnp.zeros((BINS, ROWS * WIDE), F32)
        for x in range(ROWS):
            total = jnp.where(slab == x, cross[BINS * x : BINS * (x + 1)], total)
        total = sum(total[:, LANE * i : LANE * (i + 1)] for i in range(ROWS * WIDE // LANE))
        parts.append(total[:, :WIDE] + total[:, WIDE:])
    table = jnp.concatenate(parts, axis=1)
    pieces = []
    for _ in range(3):
        piece = table.astype(BF16)
        table = table - piece.astype(F32)
        chosen = jnp.dot(left_ref[:, 0:BINS], piece, preferred_element_type=F32)
        pieces.append(chosen.astype(BF16) * right_ref[...])
    entries = lax.dot_general(
        jnp.concatenate(pieces, axis=0), spread_matrix(), (((1,), (1,)), ((), ())),
        preferred_element_type=F32,
    )
    entries = entries[0:PAIRS] + (entries[PAIRS : 2 * PAIRS] + entries[2 * PAIRS :])
    packed = jnp.concatenate(
        [entries[8 * a : 8 * (a + 1)] for a in range(GROUPS)]
        + [jnp.zeros((8, PACK - GROUPS * ENTRIES), F32)],
        axis=1,
    )
    out_ref[...] = jnp.broadcast_to(packed[None], out_ref.shape)


def backward_kernel(
    inverse_area,
    taps_ref, sums_ref, target_ref, weight_ref, left_ref, right_ref, own_ref, up_far, down_far, wa_far,
    corr_ref, out_ref, grad_ref, up_ref, down_ref, wa_ref, sem,
):
    copies = [
        pltpu.make_async_copy(up_far, up_ref, sem.at[0]),
        pltpu.make_async_copy(down_far, down_ref, sem.at[1]),
        pltpu.make_async_copy(wa_far, wa_ref, sem.at[2]),
    ]
    for copy in copies:
        copy.start()
    packed = sums_ref[0]
    for i in range(1, sums_ref.shape[0]):
        packed = packed + sums_ref[i]
    corr = inverse_area * jnp.concatenate(
        [packed[:, ENTRIES * a : ENTRIES * (a + 1)] for a in range(GROUPS)], axis=0
    )
    corr_ref[...] = corr
    grad = weight_ref[...] * (corr - target_ref[...])
    spread = spread_matrix()
    halves = []
    for piece in split2(grad):
        wide = jnp.dot(piece, spread, preferred_element_type=F32).astype(BF16)
        both = []
        for one, other in ((left_ref, right_ref), (right_ref, left_ref)):
            both.append(
                lax.dot_general(
                    one[:, 0:BINS], wide * other[...], (((0,), (0,)), ((), ())),
                    preferred_element_type=F32,
                )
            )
        halves.append(both)

    def mask_of(ref):
        return ref[SCALES * XB :, :].astype(F32) != 0

    masks = [mask_of(own_ref)]
    totals = [jnp.zeros((XB, LANE), F32)] * (OWN // LANE)
    for s in range(SCALES):
        at = slice(WIDE * s, WIDE * (s + 1))
        mix = jnp.concatenate(
            [jnp.concatenate([ahead[:, at], behind[:, at]], axis=1) for ahead, behind in halves],
            axis=0,
        )
        zero = jnp.zeros_like(mix)
        mix = jnp.concatenate(
            [jnp.concatenate([mix, zero], axis=1), jnp.concatenate([zero, mix], axis=1)], axis=0
        ).astype(BF16)
        for n, (k, ref) in enumerate(((1, own_ref), (0, up_ref), (2, down_ref))):
            if s == 0 and n:
                copies[n - 1].wait()
                masks.append(mask_of(ref))
            mask = masks[n]
            g = ref[XB * s : XB * (s + 1), :]
            ahead = [pltpu.roll(g, EDGE - l, 1) for l in range(LAGS)]
            behind = ahead[:1] + [pltpu.roll(g, EDGE + l, 1) for l in range(1, LAGS)]
            for x in range(0, ROWS, 2):
                maps = jnp.concatenate(
                    [v[BINS * y : BINS * (y + 1)] for y in (x, x + 1) for v in ahead + behind], axis=0
                )
                d = jnp.dot(mix, maps, preferred_element_type=F32)
                for i in range(2):
                    v = d[2 * BINS * i : 2 * BINS * (i + 1)]
                    grad_ref[s % 2, ROWS * k + x + i] = jnp.where(mask, v[:BINS] + v[BINS:], 0.0)
        columns = []
        for c in range(WIN // LANE):
            sums = [None] * ROWS
            for k in range(3 * ROWS):
                v = grad_ref[s % 2, k, :, LANE * c : LANE * (c + 1)]
                for x in range(ROWS):
                    if 0 <= k - x < TAPS:
                        term = taps_ref[s, TAPS - 1 - (k - x)] * v
                        sums[x] = term if sums[x] is None else sums[x] + term
            columns.append(jnp.concatenate(sums, axis=0))
        rows = jnp.concatenate(columns, axis=1)
        if s == 0:
            copies[2].wait()
        tiles = banded([rows[:, LANE * c : LANE * (c + 2)] for c in range(OWN // LANE)], wa_ref[s])
        totals = [total + tile for total, tile in zip(totals, tiles)]
    for c, total in enumerate(totals):
        for x in range(ROWS):
            at = pl.ds(ROWS * c + x, BINS, stride=ROWS * OWN // LANE)
            out_ref[at, :] = total[BINS * x : BINS * (x + 1)]


def struct(shape, dtype):
    return jax.ShapeDtypeStruct(shape, dtype)


VMEM = pl.BlockSpec(memory_space=pltpu.VMEM)
HBM = pl.BlockSpec(memory_space=pltpu.HBM)
COLUMN = (SCALES, 2 * LANE, 2 * LANE)
MAPS = (SCALES * XB + BINS, WIN)


def far(v):
    return pltpu.with_memory_space_constraint(v, pltpu.HBM)


def limit(mib):
    return pltpu.CompilerParams(vmem_limit_bytes=mib * 1024 * 1024)


def cost(flops, moved):
    return pl.CostEstimate(flops=flops, bytes_accessed=moved, transcendentals=0)


def matrices(filter_taps, bin_pairs):
    pairs = jnp.pad(bin_pairs, ((0, PAIRS - bin_pairs.shape[0]), (0, 0)), constant_values=-1)
    column = struct(COLUMN, BF16)
    return pl.pallas_call(
        matrices_kernel,
        in_specs=[SMEM, VMEM],
        out_shape=(
            struct((2, SCALES, ROWS, 3 * XB), F32),
            column,
            column,
            struct((PAIRS, TABLE), BF16),
            struct((PAIRS, TABLE), BF16),
            pltpu.HBM(COLUMN, BF16),
            pltpu.HBM(COLUMN, BF16),
            pltpu.HBM(COLUMN, BF16),
        ),
        out_specs=[VMEM] * 5 + [HBM] * 3,
        scratch_shapes=[pltpu.VMEM(COLUMN, BF16), pltpu.SemaphoreType.DMA((3,))],
        compiler_params=limit(32),
        cost_estimate=cost(20_000_000, 4_000_000),
        name="matrices",
    )(filter_taps, pairs)


def scratch():
    return [
        pltpu.VMEM((6 * XB, WIN), BF16),
        pltpu.VMEM((SCALES * XB, 6 * XB), BF16),
        pltpu.VMEM((SCALES * XB, WIN), F32),
    ]


def forward(strips, row, w, wh, left, right, copies):
    return pl.pallas_call(
        forward_kernel,
        out_shape=(struct(MAPS, BF16), struct((copies, 8, PACK), F32)),
        scratch_shapes=scratch(),
        compiler_params=limit(32),
        name="forward",
    )(*strips, row, w, wh, left, right)


def beside(strips, row, w, wh):
    return pl.pallas_call(
        beside_kernel,
        in_specs=[VMEM] * 4 + [HBM] * 2,
        out_specs=HBM,
        out_shape=pltpu.HBM(MAPS, BF16),
        scratch_shapes=scratch()
        + [
            pltpu.VMEM(COLUMN, BF16),
            pltpu.VMEM(COLUMN, BF16),
            pltpu.VMEM(MAPS, BF16),
            pltpu.SemaphoreType.DMA((3,)),
        ],
        compiler_params=limit(32),
        cost_estimate=cost(2_000_000_000, 8_000_000),
        name="beside",
    )(*strips, row, far(w), far(wh))


def backward(inverse_area, taps, sums, target, weight, left, right, wa, above, own, below):
    return pl.pallas_call(
        lambda *refs: backward_kernel(inverse_area, *refs),
        in_specs=[SMEM] + [VMEM] * 6 + [HBM] * 3,
        out_shape=(struct((PAIRS, ENTRIES), F32), struct((XB * OWN // LANE, LANE), F32)),
        scratch_shapes=[
            pltpu.VMEM((2, 3 * ROWS, BINS, WIN), F32),
            pltpu.VMEM(MAPS, BF16),
            pltpu.VMEM(MAPS, BF16),
            pltpu.VMEM(COLUMN, BF16),
            pltpu.SemaphoreType.DMA((3,)),
        ],
        compiler_params=limit(32),
        name="backward",
    )(taps, sums, target, weight, left, right, own, far(above), far(below), far(wa))


def per_device(lensing_maps, filter_taps, survey_mask, bin_pairs, target_corr, pair_weight):
    strip = lensing_maps[0]
    rows, cols = strip.shape
    bins = lax.axis_size("bin")
    sky = lax.axis_size("sky")
    pairs = bin_pairs.shape[0]
    inverse_area = 1.0 / (rows * sky * cols)
    down_perm = [(i, i + 1) for i in range(sky - 1)]
    up_perm = [(i + 1, i) for i in range(sky - 1)]

    def padded(v):
        return jnp.pad(v.reshape(pairs, ENTRIES), ((0, PAIRS - pairs), (0, 0)))

    windows = pl.pallas_call(
        windows_kernel,
        out_shape=struct((XB, WIN), BF16),
        compiler_params=limit(60),
        name="windows",
    )(strip, survey_mask)
    own = lax.all_to_all(windows, "bin", 0, 0, tiled=True)
    made = matrices(filter_taps, bin_pairs)
    own, (row, w, wh, left, right, w_far, wh_far, wa) = lax.optimization_barrier((own, made))
    above = lax.ppermute(own, "sky", down_perm)
    below = lax.ppermute(own, "sky", up_perm)
    above2 = lax.ppermute(own, "sky", [(i, i + 2) for i in range(sky - 2)])
    below2 = lax.ppermute(own, "sky", [(i + 2, i) for i in range(sky - 2)])
    g, partial = forward((above, own, below), row, w, wh, left, right, sky)
    g_above = beside((above2, above, own), row, w_far, wh_far)
    g_below = beside((own, below, below2), row, w_far, wh_far)
    partial = lax.all_to_all(partial, "sky", 0, 0, tiled=True)
    partial = jnp.broadcast_to(jnp.sum(partial, axis=0)[None], (bins,) + partial.shape[1:])
    partial = lax.all_to_all(partial, "bin", 0, 0, tiled=True)
    corr, tile_grad = backward(
        inverse_area, filter_taps, partial, padded(target_corr), padded(pair_weight),
        left, right, wa, g_above, g, g_below,
    )
    back = lax.all_to_all(tile_grad, "bin", 0, 0, tiled=True)
    map_grad = jnp.transpose(back.reshape(cols // LANE, rows, LANE), (1, 0, 2)).reshape(1, rows, cols)
    return (corr[:pairs].reshape(target_corr.shape), map_grad)


def solution(mesh):
    placed = (P("bin", "sky", None), P(), P("sky", None), P(), P(), P())
    return jax.shard_map(
        per_device,
        mesh=mesh,
        in_specs=placed,
        out_specs=(P(), P("bin", "sky", None)),
        check_vma=False,
    )
```
